512 devices in a mesh: section: 16 (over x, y_lo, core), ctx: 32 (over z, y_hi).
Axes of the slice: x: 4, y: 8 (y_hi: 4, y_lo: 2; y = y_hi * 2 + y_lo), z: 8, core: 2. Of those that a mesh axis runs over, the one named last changes fastest.
Arguments:
- queries: bfloat16 [16, 4096, 4096], P('section', 'ctx')
- key_values: bfloat16 [16, 4096, 2, 512], P('section', 'ctx')
- token_pos: int32 [4096], P('ctx'), may hold values from 0 to 4095, as said below
- layer_of_section: int32 [16], replicated, may hold values from 0 to 15, each once
Outputs:
- attended: bfloat16 [16, 4096, 4096], P('section', 'ctx')
The draws below stay inside these ranges and needn't reach their ends.
Inputs may be any that keep to these rules, and one draw needn't show every extreme that they name: `token_pos`: each aligned block of 64 entries holds 64 consecutive positions rising by one; all entries together are each position of 0 to 4095 once.
All inputs are finite; a program needn't handle non-finite values.
Results may differ from the reference program's by a relative error of at most 0.0065.
Values may be sent and summed in bfloat16 or wider, within the bound.
No kernel may reach another device: no remote copies, remote signals or barrier semaphores. Data moves between devices by JAX's collectives and lax.ppermute only.
A program may use at most 64 MiB of HBM per device.

```python
import jax
import jax.numpy as jnp
from jax import lax

H = 32
KVH = 4
HD = 128
WARM = 2
GROUP = 8
BLOCK = 64
TOKENS = 4096
LAYERS = 16


def block_layout(key):
    block_count = TOKENS // BLOCK
    block_order = jax.random.permutation(jax.random.fold_in(key, 11), block_count)
    layout = block_order[:, None] * BLOCK + jnp.arange(BLOCK)[None, :]
    return layout.reshape(TOKENS).astype(jnp.int32)


def draw_token_pos(key, part):
    layout = block_layout(key)
    return layout


def draw_queries(key, part):
    key = jax.random.fold_in(key, 5)
    full_shape = (LAYERS, TOKENS, KVH, GROUP, HD)
    sample = jax.random.normal(key, full_shape, jnp.float32)
    return sample.reshape(LAYERS, TOKENS, H * HD).astype(jnp.bfloat16)


def draw_key_values(key, part):
    key = jax.random.fold_in(key, 7)
    full_shape = (LAYERS, TOKENS, 2, KVH, HD)
    sample = jax.random.normal(key, full_shape, jnp.float32)
    return sample.reshape(LAYERS, TOKENS, 2, KVH * HD).astype(jnp.bfloat16)


def setup_inputs(seed: int = 0) -> dict:
    key_list = jax.random.split(jax.random.key(seed), 5)
    return {
        "queries": draw_queries(jax.random.fold_in(key_list[4], 71), 0),
        "key_values": draw_key_values(jax.random.fold_in(key_list[4], 71), 0),
        "token_pos": draw_token_pos(jax.random.fold_in(key_list[4], 71), 0),
        "layer_of_section": jax.random.permutation(key_list[3], LAYERS).astype(jnp.int32),
    }


masked_score = -1e30


def attend(section_queries, key_rows, value_rows, positions):
    group_size = H // KVH
    block_rows = 512 if TOKENS % 512 == 0 else TOKENS
    block_count = TOKENS // block_rows
    score_scale = HD ** -0.5
    query_blocks = section_queries.reshape(block_count, block_rows, KVH, group_size, HD)
    position_blocks = positions.reshape(block_count, block_rows)

    def one_block(block_args):
        query_block, query_pos = block_args
        scores = jnp.einsum("qkgd,ckd->qkgc", query_block.astype(jnp.float32), key_rows.astype(jnp.float32)) * score_scale
        visible = (positions[None, :] <= query_pos[:, None])[:, None, None, :]
        scores = jnp.where(visible, scores, masked_score)
        row_max = jnp.max(scores, axis=-1, keepdims=True)
        weights = jnp.where(visible, jnp.exp(scores - row_max), 0.0)
        denominator = jnp.sum(weights, axis=-1)
        rounded = lax.optimization_barrier(weights.astype(jnp.bfloat16))
        mixed_rows = jnp.einsum("qkgc,ckd->qkgd", rounded.astype(jnp.float32), value_rows.astype(jnp.float32))
        return (mixed_rows / denominator[..., None]).astype(jnp.bfloat16)

    return lax.map(one_block, (query_blocks, position_blocks)).reshape(TOKENS, H * HD)


def reference(queries, key_values, token_pos, layer_of_section):
    layer_ids = jnp.arange(LAYERS, dtype=jnp.int32)
    top_section = jnp.sum(jnp.where(layer_of_section == LAYERS - 1, layer_ids, 0)).astype(jnp.int32)
    top_rows = lax.dynamic_index_in_dim(key_values, top_section, 0, keepdims=False)

    def per_section(section_args):
        section_queries, own_rows, layer_id = section_args
        source = jnp.where(layer_id < WARM, own_rows, top_rows)
        key_rows = source[:, 0].reshape(TOKENS, KVH, HD)
        value_rows = source[:, 1].reshape(TOKENS, KVH, HD)
        return attend(section_queries, key_rows, value_rows, token_pos)

    return lax.map(per_section, (queries, key_values, layer_of_section))
```

```python
import functools

import jax
import jax.numpy as jnp
from jax import lax
from jax.experimental import pallas as pl
from jax.experimental.pallas import tpu as pltpu
from jax.sharding import Mesh, PartitionSpec as P

H = 32
KVH = 4
HD = 128
GROUP = 8
BLOCK = 64
WARM = 2
ROWS = 128
POS_ROWS = 16
SHARD = 2 * KVH * ROWS + POS_ROWS
MASKED = -1e30
SCALE = 1.4426950408889634 / HD**0.5


def attend_body(shards, first, last, *refs):
    it = iter(refs)
    q_ref, pos_ref = next(it), next(it)
    keys, values, caps = [], [], []
    lane = (lax.broadcasted_iota(jnp.int32, (1, ROWS), 1) % BLOCK).astype(jnp.float32)
    for n in shards:
        k_ref, v_ref, p_ref = next(it), next(it), next(it)
        for i in range(n):
            keys.append(k_ref[i])
            values.append(v_ref[i])
            key_pos = p_ref[i][0:1, :].astype(jnp.float32) * BLOCK + lane
            caps.append(jnp.where(key_pos <= pos_ref[...], jnp.inf, MASKED))
    k = jnp.concatenate(keys, axis=0)
    count = k.shape[0]
    v = jnp.concatenate(values, axis=0)
    v = jnp.concatenate([v, jnp.ones((count, HD), jnp.bfloat16)], axis=1)
    cap = jnp.concatenate(caps, axis=1).astype(jnp.float32)
    if not first:
        m_in, l_in, a_in = next(it), next(it), next(it)
    outs = list(it)
    for g in range(GROUP):
        cols = slice(g * HD, (g + 1) * HD)
        s = lax.dot_general(
            q_ref[:, cols], k, (((1,), (1,)), ((), ())), preferred_element_type=jnp.float32
        )
        s = jnp.minimum(s, cap)
        top = jnp.max(s, axis=1, keepdims=True)
        if first:
            m = jnp.broadcast_to(top, (ROWS, HD))
        else:
            m_old = m_in[:, cols]
            m = jnp.maximum(m_old, top)
        wide = jnp.concatenate([m] * (count // HD), axis=1)
        w = jnp.exp2((s - wide) * SCALE).astype(jnp.bfloat16)
        o = lax.dot_general(
            w, v, (((1,), (0,)), ((), ())), preferred_element_type=jnp.float32
        )
        acc, den = o[:, :HD], o[:, HD:]
        if not first:
            f = jnp.exp2((m_old - m) * SCALE)
            acc = acc + f * a_in[:, cols]
            den = den + f * l_in[:, cols]
        if last:
            outs[0][:, cols] = (acc / den).astype(jnp.bfloat16)
        else:
            outs[0][:, cols] = m
            outs[1][:, cols] = den
            outs[2][:, cols] = acc


def attend(q, pos, blocks, state, last):
    shards = tuple(b.shape[0] for b in blocks)
    wide = pl.BlockSpec((ROWS, GROUP * HD), lambda h: (0, h))
    in_specs = [wide, pl.BlockSpec((ROWS, 1), lambda h: (0, 0))]
    args = [q, pos]
    for b in blocks:
        n = b.shape[0]
        in_specs += [
            pl.BlockSpec((n, ROWS, HD), lambda h: (0, h, 0)),
            pl.BlockSpec((n, ROWS, HD), lambda h: (0, KVH + h, 0)),
            pl.BlockSpec((n, POS_ROWS, HD), lambda h: (0, 2 * KVH * ROWS // POS_ROWS, 0)),
        ]
        args += [b, b, b]
    if state is not None:
        in_specs += [wide] * 3
        args += list(state)
    kept = jax.ShapeDtypeStruct((ROWS, H * HD), jnp.float32)
    done = jax.ShapeDtypeStruct((ROWS, H * HD), jnp.bfloat16)
    count = sum(shards) * ROWS
    return pl.pallas_call(
        functools.partial(attend_body, shards, state is None, last),
        grid=(KVH,),
        in_specs=in_specs,
        out_specs=wide if last else [wide] * 3,
        out_shape=done if last else [kept] * 3,
        compiler_params=pltpu.CompilerParams(vmem_limit_bytes=40 << 20),
        cost_estimate=pl.CostEstimate(
            flops=4 * ROWS * H * count * HD,
            bytes_accessed=8 << 20,
            transcendentals=ROWS * H * count,
        ),
        name="attend",
    )(*args)


def turn(value, axis, size, shift):
    return lax.ppermute(value, axis, [(i, (i + shift) % size) for i in range(size)])


def per_device(sizes, queries, key_values, token_pos, layer_of_section):
    nx, nyl, nz, nyh = sizes["x"], sizes["yl"], sizes["z"], sizes["yh"]
    layers = layer_of_section.shape[0]
    section = lax.axis_index(("x", "yl", "core"))
    ids = jnp.arange(layers, dtype=jnp.int32)
    layer = jnp.sum(jnp.where(ids == section, layer_of_section, 0))
    own = key_values[0].reshape(ROWS, 2 * KVH, HD).transpose(1, 0, 2).reshape(2 * KVH * ROWS, HD)
    top = jnp.where(layer == layers - 1, own, 0).astype(jnp.bfloat16)
    top = top + turn(top, "core", 2, 1)
    top = top + turn(top, "yl", nyl, 1)
    parts = [turn(top, "x", nx, shift) for shift in range(1, nx)]
    for part in parts:
        top = top + part
    rows = jnp.where(layer < WARM, own, top)
    block_id = jnp.broadcast_to((token_pos // BLOCK).astype(jnp.bfloat16)[None, :], (POS_ROWS, ROWS))
    shard = jnp.concatenate([rows, block_id], axis=0)
    line = jnp.stack([shard] + [turn(shard, "yh", nyh, shift) for shift in range(1, nyh)])
    q = queries[0]
    pos = token_pos.astype(jnp.float32)[:, None]
    up, down = turn(line, "z", nz, 1), turn(line, "z", nz, -1)
    state = attend(q, pos, [line], None, False)
    for _ in range(nz // 2 - 2):
        nup, ndown = turn(up, "z", nz, 1), turn(down, "z", nz, -1)
        state = attend(q, pos, [up, down], state, False)
        up, down = nup, ndown
    half = nyh // 2
    last_up, last_down = turn(up[:half], "z", nz, 1), turn(down[half:], "z", nz, -1)
    state = attend(q, pos, [up, down], state, False)
    out = attend(q, pos, [last_up, last_down], state, True)
    return out[None]


def solution(mesh):
    sizes = {"x": 4, "yl": 2, "core": 2, "z": 8, "yh": 4}
    fine = Mesh(mesh.devices.reshape(tuple(sizes.values())), tuple(sizes))
    section, ctx = ("x", "yl", "core"), ("z", "yh")
    in_specs = (P(section, ctx, None), P(section, ctx, None, None), P(ctx), P())
    return jax.shard_map(
        functools.partial(per_device, sizes),
        mesh=fine,
        in_specs=in_specs,
        out_specs=P(section, ctx, None),
        check_vma=False,
    )
```

```python
import functools

import jax
import jax.numpy as jnp
from jax import lax
from jax.experimental import pallas as pl
from jax.experimental.pallas import tpu as pltpu
from jax.sharding import Mesh, PartitionSpec as P

H = 32
KVH = 4
HD = 128
GROUP = 8
BLOCK = 64
WARM = 2
ROWS = 128
POS_ROWS = 16
MASKED = -1e30
SCALE = 1.4426950408889634 / HD**0.5


def attend_body(shards, first, last, *refs):
    it = iter(refs)
    q_ref, pos_ref = next(it), next(it)
    keys, values, caps = [], [], []
    lane = (lax.broadcasted_iota(jnp.int32, (1, ROWS), 1) % BLOCK).astype(jnp.float32)
    for n in shards:
        k_ref, v_ref, p_ref = next(it), next(it), next(it)
        for i in range(n):
            keys.append(k_ref[i])
            values.append(v_ref[i])
            key_pos = p_ref[i][0:1, :].astype(jnp.float32) * BLOCK + lane
            caps.append(jnp.where(key_pos <= pos_ref[...], jnp.inf, MASKED))
    k = jnp.concatenate(keys, axis=0)
    count = k.shape[0]
    v = jnp.concatenate(values, axis=0)
    v = jnp.concatenate([v, jnp.ones((count, HD), jnp.bfloat16)], axis=1)
    cap = jnp.concatenate(caps, axis=1).astype(jnp.float32)
    if not first:
        m_in, l_in, a_in = next(it), next(it), next(it)
    outs = list(it)
    for g in range(GROUP):
        cols = slice(g * HD, (g + 1) * HD)
        s = lax.dot_general(
            q_ref[:, cols], k, (((1,), (1,)), ((), ())), preferred_element_type=jnp.float32
        )
        s = jnp.minimum(s, cap)
        top = jnp.max(s, axis=1, keepdims=True)
        if first:
            m = jnp.broadcast_to(top, (ROWS, HD))
        else:
            m_old = m_in[:, cols]
            m = jnp.maximum(m_old, top)
        wide = jnp.concatenate([m] * (count // HD), axis=1)
        w = jnp.exp2((s - wide) * SCALE).astype(jnp.bfloat16)
        o = lax.dot_general(
            w, v, (((1,), (0,)), ((), ())), preferred_element_type=jnp.float32
        )
        acc, den = o[:, :HD], o[:, HD:]
        if not first:
            f = jnp.exp2((m_old - m) * SCALE)
            acc = acc + f * a_in[:, cols]
            den = den + f * l_in[:, cols]
        if last:
            outs[0][:, cols] = (acc / den).astype(jnp.bfloat16)
        else:
            outs[0][:, cols] = m
            outs[1][:, cols] = den
            outs[2][:, cols] = acc


def attend(q, pos, blocks, heads, offset, state, last):
    shards = tuple(b.shape[0] for b in blocks)
    wide = pl.BlockSpec((ROWS, GROUP * HD), lambda h: (0, h))
    in_specs = [
        pl.BlockSpec((ROWS, GROUP * HD), lambda h: (0, offset + h)),
        pl.BlockSpec((ROWS, 1), lambda h: (0, 0)),
    ]
    args = [q, pos]
    for b in blocks:
        n = b.shape[0]
        in_specs += [
            pl.BlockSpec((n, ROWS, HD), lambda h: (0, h, 0)),
            pl.BlockSpec((n, ROWS, HD), lambda h: (0, heads + h, 0)),
            pl.BlockSpec((n, POS_ROWS, HD), lambda h: (0, 2 * heads * ROWS // POS_ROWS, 0)),
        ]
        args += [b, b, b]
    if state is not None:
        in_specs += [wide] * 3
        args += list(state)
    kept = jax.ShapeDtypeStruct((ROWS, heads * GROUP * HD), jnp.float32)
    done = jax.ShapeDtypeStruct((ROWS, heads * GROUP * HD), jnp.bfloat16)
    count = sum(shards) * ROWS
    return pl.pallas_call(
        functools.partial(attend_body, shards, state is None, last),
        grid=(heads,),
        in_specs=in_specs,
        out_specs=wide if last else [wide] * 3,
        out_shape=done if last else [kept] * 3,
        compiler_params=pltpu.CompilerParams(vmem_limit_bytes=40 << 20),
        cost_estimate=pl.CostEstimate(
            flops=4 * ROWS * heads * GROUP * count * HD,
            bytes_accessed=8 << 20,
            transcendentals=ROWS * heads * GROUP * count,
        ),
        name="attend",
    )(*args)


def turn(value, axis, size, shift):
    return lax.ppermute(value, axis, [(i, (i + shift) % size) for i in range(size)])


def with_ids(rows, token_pos):
    ids = (token_pos // BLOCK).astype(jnp.bfloat16)[None, :]
    return jnp.concatenate([rows, jnp.broadcast_to(ids, (POS_ROWS, ROWS))], axis=0)


def per_device(sizes, queries, key_values, token_pos, layer_of_section):
    nz, nyh = sizes["z"], sizes["yh"]
    axes = ("x", "yl", "core")
    layers = layer_of_section.shape[0]
    section = lax.axis_index(axes)
    ids = jnp.arange(layers, dtype=jnp.int32)
    layer = jnp.sum(jnp.where(ids == section, layer_of_section, 0))
    top_section = jnp.sum(jnp.where(layer_of_section == layers - 1, ids, 0))
    own = key_values[0].reshape(ROWS, 2, KVH, HD).transpose(2, 1, 0, 3)
    pieces = own.reshape(layers, 2 * KVH * ROWS // layers, HD)
    piece = lax.dynamic_index_in_dim(lax.all_to_all(pieces, axes, 0, 0), top_section, 0, True)
    top = lax.all_to_all(jnp.broadcast_to(piece, pieces.shape), axes, 0, 0)
    rows = jnp.where(layer < WARM, own, top.reshape(own.shape))
    side = KVH - 1
    ring_rows = rows[:side].transpose(1, 0, 2, 3).reshape(2 * side * ROWS, HD)
    side_rows = rows[side:].transpose(1, 0, 2, 3).reshape(2 * (KVH - side) * ROWS, HD)
    q = queries[0]
    pos = token_pos.astype(jnp.float32)[:, None]
    beside = lax.all_gather(with_ids(side_rows, token_pos), ("z", "yh"), axis=0)
    shard = with_ids(ring_rows, token_pos)
    line = jnp.stack([shard] + [turn(shard, "yh", nyh, shift) for shift in range(1, nyh)])

    def part(blocks, state, last=False):
        return attend(q, pos, blocks, side, 0, state, last)

    held, state = [line], None
    up = down = line
    for _ in range(nz // 2 - 1):
        up, down = turn(up, "z", nz, 1), turn(down, "z", nz, -1)
        state = part(held, state)
        up, down, state = lax.optimization_barrier((up, down, state))
        held = [up, down]
    half = nyh // 2
    last_up, last_down = turn(up[:half], "z", nz, 1), turn(down[half:], "z", nz, -1)
    state = part(held, state)
    side_out = attend(q, pos, [beside], KVH - side, side, None, True)
    last_up, last_down, state, side_out = lax.optimization_barrier((last_up, last_down, state, side_out))
    out = part([last_up, last_down], state, True)
    return jnp.concatenate([out, side_out], axis=1)[None]


def solution(mesh):
    sizes = {"x": 4, "yl": 2, "core": 2, "z": 8, "yh": 4}
    fine = Mesh(mesh.devices.reshape(tuple(sizes.values())), tuple(sizes))
    section, ctx = ("x", "yl", "core"), ("z", "yh")
    in_specs = (P(section, ctx, None), P(section, ctx, None, None), P(ctx), P())
    return jax.shard_map(
        functools.partial(per_device, sizes),
        mesh=fine,
        in_specs=in_specs,
        out_specs=P(section, ctx, None),
        check_vma=False,
    )
```

```python
import functools

import jax
import jax.numpy as jnp
from jax import lax
from jax.experimental import pallas as pl
from jax.experimental.pallas import tpu as pltpu
from jax.sharding import Mesh, PartitionSpec as P

H = 32
KVH = 4
HD = 128
BLOCK = 64
WARM = 2
LAYERS = 16
ROWS = 128
HEADS = H // LAYERS
WIDE = HEADS * HD
POS_ROWS = 16
MASKED = -1e30
SCALE = 1.4426950408889634 / HD**0.5
SECTION = ("x", "yl", "core")


def attend_body(shards, first, last, *refs):
    it = iter(refs)
    next(it)
    q_ref, pos_ref = next(it), next(it)
    blocks = [(next(it), next(it), next(it)) for _ in shards]
    if not first:
        m_in, l_in, a_in = next(it), next(it), next(it)
    outs = [next(it)] if last else [next(it), next(it), next(it)]
    k, v, cap = it
    step = pl.program_id(0)
    count = k.shape[0]

    @pl.when(step == 0)
    def _():
        lane = (lax.broadcasted_iota(jnp.int32, (1, ROWS), 1) % BLOCK).astype(jnp.float32)
        v[:, HD:] = jnp.ones((count, HD), jnp.bfloat16)
        at = 0
        for n, (_, _, p_ref) in zip(shards, blocks):
            for i in range(n):
                key_pos = p_ref[i][0:1, :].astype(jnp.float32) * BLOCK + lane
                cap[:, at : at + ROWS] = jnp.where(key_pos <= pos_ref[...], jnp.inf, MASKED)
                at += ROWS

    @pl.when((step == 0) | (step == WARM))
    def _():
        at = 0
        for n, (k_ref, v_ref, _) in zip(shards, blocks):
            for i in range(n):
                k[at : at + ROWS, :] = k_ref[i]
                v[at : at + ROWS, :HD] = v_ref[i]
                at += ROWS

    for g in range(HEADS):
        cols = slice(g * HD, (g + 1) * HD)
        s = lax.dot_general(
            q_ref[:, cols], k[...], (((1,), (1,)), ((), ())), preferred_element_type=jnp.float32
        )
        s = jnp.minimum(s, cap[...])
        top = jnp.max(s, axis=1, keepdims=True)
        if first:
            m = jnp.broadcast_to(top, (ROWS, HD))
        else:
            m_old = m_in[:, cols]
            m = jnp.maximum(m_old, top)
        wide = jnp.concatenate([m] * (count // HD), axis=1)
        w = jnp.exp2((s - wide) * SCALE).astype(jnp.bfloat16)
        o = lax.dot_general(
            w, v[...], (((1,), (0,)), ((), ())), preferred_element_type=jnp.float32
        )
        acc, den = o[:, :HD], o[:, HD:]
        if not first:
            f = jnp.exp2((m_old - m) * SCALE)
            acc = acc + f * a_in[:, cols]
            den = den + f * l_in[:, cols]
        if last:
            outs[0][:, cols] = (acc / den).astype(jnp.bfloat16)
        else:
            outs[0][:, cols] = m
            outs[1][:, cols] = den
            outs[2][:, cols] = acc


def attend(order, q, pos, blocks, state, last):
    shards = tuple(b.shape[0] for b in blocks)
    count = sum(shards) * ROWS
    picked = pl.BlockSpec((None, ROWS, WIDE), lambda i, order: (order[i], 0, 0))
    kept = pl.BlockSpec((None, ROWS, WIDE), lambda i, order: (i, 0, 0))
    in_specs = [picked, pl.BlockSpec((ROWS, 1), lambda i, order: (0, 0))]
    args = [q, pos]
    for b in blocks:
        n = b.shape[0]
        in_specs += [
            pl.BlockSpec((n, ROWS, HD), lambda i, order: (0, jnp.where(i < WARM, 2, 0), 0)),
            pl.BlockSpec((n, ROWS, HD), lambda i, order: (0, jnp.where(i < WARM, 3, 1), 0)),
            pl.BlockSpec((n, POS_ROWS, HD), lambda i, order: (0, 4 * ROWS // POS_ROWS, 0)),
        ]
        args += [b, b, b]
    if state is not None:
        in_specs += [kept] * 3
        args += list(state)
    held = jax.ShapeDtypeStruct((LAYERS, ROWS, WIDE), jnp.float32)
    done = jax.ShapeDtypeStruct((LAYERS + 1, ROWS, WIDE), jnp.bfloat16)
    return pl.pallas_call(
        functools.partial(attend_body, shards, state is None, last),
        grid_spec=pltpu.PrefetchScalarGridSpec(
            num_scalar_prefetch=1,
            grid=(LAYERS,),
            in_specs=in_specs,
            out_specs=picked if last else [kept] * 3,
            scratch_shapes=[
                pltpu.VMEM((count, HD), jnp.bfloat16),
                pltpu.VMEM((count, 2 * HD), jnp.bfloat16),
                pltpu.VMEM((ROWS, count), jnp.float32),
            ],
        ),
        out_shape=done if last else [held] * 3,
        compiler_params=pltpu.CompilerParams(vmem_limit_bytes=40 << 20),
        cost_estimate=pl.CostEstimate(
            flops=4 * ROWS * H * count * HD,
            bytes_accessed=8 << 20,
            transcendentals=ROWS * H * count,
        ),
        name="attend",
    )(order, *args)


def turn(value, axis, size, shift):
    return lax.ppermute(value, axis, [(i, (i + shift) % size) for i in range(size)])


def pick(slabs, index):
    return lax.dynamic_index_in_dim(slabs, index, 0, keepdims=False)


def per_device(sizes, queries, key_values, token_pos, layer_of_section):
    nz, nyh = sizes["z"], sizes["yh"]
    core = lax.axis_index("core")
    ids = jnp.arange(LAYERS, dtype=jnp.int32)
    holder = jnp.sum(jnp.where(layer_of_section[None, :] == ids[:, None], ids[None, :], 0), axis=1)
    warm, other_warm = pick(holder, core), pick(holder, 1 - core)
    heads = key_values[0].reshape(ROWS, 2, KVH, HD).transpose(2, 1, 0, 3)
    pieces = jnp.broadcast_to(
        heads.reshape(KVH, 1, 2 * ROWS, HD), (KVH, LAYERS // KVH, 2 * ROWS, HD)
    ).reshape(LAYERS, 2 * ROWS, HD)
    pieces = lax.all_to_all(pieces, SECTION, 0, 0)
    block_ids = jnp.broadcast_to((token_pos // BLOCK).astype(jnp.bfloat16)[None, :], (POS_ROWS, ROWS))
    shard = jnp.concatenate([pick(pieces, holder[LAYERS - 1]), pick(pieces, warm), block_ids], axis=0)
    q = queries[0].reshape(ROWS, LAYERS, WIDE).transpose(1, 0, 2)
    q, shard = lax.optimization_barrier((q, shard))
    q = lax.all_to_all(q, SECTION, 0, 0)
    q = jnp.concatenate([q, turn(pick(q, other_warm), "core", 2, 1)[None]], axis=0)
    order = jnp.concatenate([jnp.stack([warm, LAYERS]), holder[WARM:]]).astype(jnp.int32)
    pos = token_pos.astype(jnp.float32)[:, None]
    line = jnp.stack([shard] + [turn(shard, "yh", nyh, shift) for shift in range(1, nyh)])

    def part(blocks, state, last=False):
        return attend(order, q, pos, blocks, state, last)

    held, state = [line], None
    up = down = line
    for _ in range(nz // 2 - 1):
        up, down = turn(up, "z", nz, 1), turn(down, "z", nz, -1)
        state = part(held, state)
        up, down, state = lax.optimization_barrier((up, down, state))
        held = [up, down]
    half = nyh // 2
    last_up, last_down = turn(up[:half], "z", nz, 1), turn(down[half:], "z", nz, -1)
    state = part(held, state)
    last_up, last_down, state = lax.optimization_barrier((last_up, last_down, state))
    out = part([last_up, last_down], state, True)
    back = turn(out[LAYERS], "core", 2, 1)
    out = jnp.where(ids[:, None, None] == other_warm, back[None], out[:LAYERS])
    out = lax.all_to_all(out, SECTION, 0, 0)
    return out.transpose(1, 0, 2).reshape(1, ROWS, H * HD)


def solution(mesh):
    sizes = {"x": 4, "yl": 2, "core": 2, "z": 8, "yh": 4}
    fine = Mesh(mesh.devices.reshape(tuple(sizes.values())), tuple(sizes))
    ctx = ("z", "yh")
    in_specs = (P(SECTION, ctx, None), P(SECTION, ctx, None, None), P(ctx), P())
    return jax.shard_map(
        functools.partial(per_device, sizes),
        mesh=fine,
        in_specs=in_specs,
        out_specs=P(SECTION, ctx, None),
        check_vma=False,
    )
```

```python
import functools

import jax
import jax.numpy as jnp
from jax import lax
from jax.experimental import pallas as pl
from jax.experimental.pallas import tpu as pltpu
from jax.sharding import Mesh, PartitionSpec as P

H = 32
KVH = 4
HD = 128
BLOCK = 64
WARM = 2
LAYERS = 16
ROWS = 128
HEADS = H // LAYERS
WIDE = HEADS * HD
SLABS = 8
POS_ROWS = 16
MASKED = -1e30
SCALE = 1.4426950408889634 / HD**0.5
SECTION = ("x", "yl", "core")


def attend_body(shards, first, last, *refs):
    it = iter(refs)
    warm_ref, q_ref, pos_ref = next(it), next(it), next(it)
    blocks = [next(it) for _ in shards]
    if not first:
        m_in, l_in, a_in = next(it), next(it), next(it)
    outs = [next(it)] if last else [next(it), next(it), next(it)]
    k, v, cap = it
    step = pl.program_id(0)
    count = k.shape[1]

    @pl.when(step == 0)
    def _():
        row = lax.broadcasted_iota(jnp.int32, (BLOCK, ROWS), 0).astype(jnp.float32)
        at = 0
        for n, ref in zip(shards, blocks):
            for i in range(n):
                for source in range(2):
                    base = source * 2 * ROWS
                    k[source, at : at + ROWS, :] = ref[i, base : base + ROWS]
                    v[source, :HD, at : at + ROWS] = ref[i, base + ROWS : base + 2 * ROWS]
                ids = ref[i, 4 * ROWS : 4 * ROWS + POS_ROWS].astype(jnp.float32)
                for part in range(ROWS // BLOCK):
                    key_pos = ids[0:1, part * BLOCK : part * BLOCK + 1] * BLOCK + row
                    rows = slice(at + part * BLOCK, at + (part + 1) * BLOCK)
                    cap[rows, :] = jnp.where(key_pos <= pos_ref[...], jnp.inf, MASKED)
                at += ROWS
        for source in range(2):
            v[source, HD:, :] = jnp.ones((POS_ROWS, count), jnp.bfloat16)

    def scores(j):
        q = jnp.concatenate([q_ref[j][:, h * HD : (h + 1) * HD] for h in range(HEADS)], axis=0)
        source = warm_ref[step * SLABS + j]
        return lax.dot_general(
            k[source], q, (((1,), (1,)), ((), ())), preferred_element_type=jnp.float32
        )

    def absorb(j, s):
        s = jnp.minimum(s, jnp.concatenate([cap[...]] * HEADS, axis=1))
        m = jnp.max(s, axis=0, keepdims=True)
        if not first:
            m_old = m_in[j, 0:1, :]
            m = jnp.maximum(m_old, m)
        w = jnp.exp2((s - m) * SCALE).astype(jnp.bfloat16)
        o = lax.dot_general(
            v[warm_ref[step * SLABS + j]],
            w,
            (((1,), (0,)), ((), ())),
            preferred_element_type=jnp.float32,
        )
        acc, den = o[:HD], o[HD : HD + 8]
        if not first:
            f = jnp.exp2((m_old - m) * SCALE)
            acc = acc + f * a_in[j]
            den = den + f * l_in[j]
        if last:
            done = acc / den[0:1]
            for h in range(HEADS):
                cols = slice(h * HD, (h + 1) * HD)
                outs[0][j, :, cols] = done[:, cols].T.astype(jnp.bfloat16)
        else:
            outs[0][j] = jnp.broadcast_to(m, den.shape)
            outs[1][j] = den
            outs[2][j] = acc

    s = scores(0)
    for j in range(SLABS):
        ahead = scores(j + 1) if j + 1 < SLABS else None
        absorb(j, s)
        s = ahead


def attend(warm, q, pos, blocks, state, last):
    shards = tuple(b.shape[0] for b in blocks)
    count = sum(shards) * ROWS
    slab = pl.BlockSpec((SLABS, ROWS, WIDE), lambda i, warm: (i, 0, 0))
    small = pl.BlockSpec((SLABS, 8, WIDE), lambda i, warm: (i, 0, 0))
    in_specs = [slab, pl.BlockSpec((1, ROWS), lambda i, warm: (0, 0))]
    in_specs += [pl.BlockSpec(b.shape, lambda i, warm: (0, 0, 0)) for b in blocks]
    args = [q, pos, *blocks]
    if state is not None:
        in_specs += [small, small, slab]
        args += list(state)
    one = jax.ShapeDtypeStruct((LAYERS, 8, WIDE), jnp.float32)
    acc = jax.ShapeDtypeStruct((LAYERS, HD, WIDE), jnp.float32)
    done = jax.ShapeDtypeStruct((LAYERS, ROWS, WIDE), jnp.bfloat16)
    return pl.pallas_call(
        functools.partial(attend_body, shards, state is None, last),
        grid_spec=pltpu.PrefetchScalarGridSpec(
            num_scalar_prefetch=1,
            grid=(LAYERS // SLABS,),
            in_specs=in_specs,
            out_specs=slab if last else [small, small, slab],
            scratch_shapes=[
                pltpu.VMEM((2, count, HD), jnp.bfloat16),
                pltpu.VMEM((2, HD + POS_ROWS, count), jnp.bfloat16),
                pltpu.VMEM((count, ROWS), jnp.float32),
            ],
        ),
        out_shape=done if last else [one, one, acc],
        compiler_params=pltpu.CompilerParams(vmem_limit_bytes=48 << 20),
        cost_estimate=pl.CostEstimate(
            flops=4 * ROWS * H * count * HD,
            bytes_accessed=8 << 20,
            transcendentals=ROWS * H * count,
        ),
        name="attend",
    )(warm, *args)


def turn(value, axis, size, shift):
    return lax.ppermute(value, axis, [(i, (i + shift) % size) for i in range(size)])


def pick(slabs, index):
    return lax.dynamic_index_in_dim(slabs, index, 0, keepdims=False)


def swap(slabs, index):
    other = turn(pick(slabs, index), "core", 2, 1)
    return lax.dynamic_update_index_in_dim(slabs, other, index, 0)


def per_device(sizes, queries, key_values, token_pos, layer_of_section):
    nz, nyh = sizes["z"], sizes["yh"]
    core = lax.axis_index("core")
    ids = jnp.arange(LAYERS, dtype=jnp.int32)
    holder = jnp.sum(jnp.where(layer_of_section[None, :] == ids[:, None], ids[None, :], 0), axis=1)
    warm, other_warm = pick(holder, core), pick(holder, 1 - core)
    kv = key_values[0].reshape(ROWS, 2, KVH, HD)
    heads = jnp.stack([kv[:, 0].transpose(1, 0, 2), kv[:, 1].transpose(1, 2, 0)], axis=1)
    pieces = jnp.broadcast_to(
        heads.reshape(KVH, 1, 2 * ROWS, HD), (KVH, LAYERS // KVH, 2 * ROWS, HD)
    ).reshape(LAYERS, 2 * ROWS, HD)
    pieces = lax.all_to_all(pieces, SECTION, 0, 0)
    block_ids = jnp.broadcast_to((token_pos // BLOCK).astype(jnp.bfloat16)[None, :], (POS_ROWS, ROWS))
    shard = jnp.concatenate([pick(pieces, holder[LAYERS - 1]), pick(pieces, warm), block_ids], axis=0)
    line = jnp.stack([shard] + [turn(shard, "yh", nyh, shift) for shift in range(1, nyh)])
    q = queries[0].reshape(ROWS, LAYERS, WIDE).transpose(1, 0, 2)
    q, line = lax.optimization_barrier((q, line))
    up, down = turn(line, "z", nz, 1), turn(line, "z", nz, -1)
    q = lax.all_to_all(q, SECTION, 0, 0)
    q = swap(q, other_warm)
    use_warm = ((ids == warm) | (ids == other_warm)).astype(jnp.int32)
    pos = token_pos.astype(jnp.float32)[None, :]

    def part(blocks, state, last=False):
        return attend(use_warm, q, pos, blocks, state, last)

    up, down, q = lax.optimization_barrier((up, down, q))
    held, state = [line, up, down], None
    for _ in range(nz // 2 - 2):
        up, down = turn(up, "z", nz, 1), turn(down, "z", nz, -1)
        state = part(held, state)
        up, down, state = lax.optimization_barrier((up, down, state))
        held = [up, down]
    half = nyh // 2
    last_up, last_down = turn(up[:half], "z", nz, 1), turn(down[half:], "z", nz, -1)
    state = part(held, state)
    last_up, last_down, state = lax.optimization_barrier((last_up, last_down, state))
    out = swap(part([last_up, last_down], state, True), other_warm)
    out = lax.all_to_all(out, SECTION, 0, 0)
    return out.transpose(1, 0, 2).reshape(1, ROWS, H * HD)


def solution(mesh):
    sizes = {"x": 4, "yl": 2, "core": 2, "z": 8, "yh": 4}
    fine = Mesh(mesh.devices.reshape(tuple(sizes.values())), tuple(sizes))
    ctx = ("z", "yh")
    in_specs = (P(SECTION, ctx, None), P(SECTION, ctx, None, None), P(ctx), P())
    return jax.shard_map(
        functools.partial(per_device, sizes),
        mesh=fine,
        in_specs=in_specs,
        out_specs=P(SECTION, ctx, None),
        check_vma=False,
    )
```

```python
import functools

import jax
import jax.numpy as jnp
from jax import lax
from jax.experimental import pallas as pl
from jax.experimental.pallas import tpu as pltpu
from jax.sharding import Mesh, PartitionSpec as P

H = 32
KVH = 4
HD = 128
BLOCK = 64
WARM = 2
LAYERS = 16
ROWS = 128
HEADS = H // LAYERS
WIDE = HEADS * HD
SLABS = 8
POS_ROWS = 16
MASKED = -1e30
SCALE = 1.4426950408889634 / HD**0.5
SECTION = ("x", "yl", "core")


def attend_body(shards, first, last, *refs):
    it = iter(refs)
    warm_ref, q_ref, pos_ref = next(it), next(it), next(it)
    blocks = [next(it) for _ in shards]
    if not first:
        m_in, l_in, a_in = next(it), next(it), next(it)
    outs = [next(it)] if last else [next(it), next(it), next(it)]
    k, v, cap = it
    count = k.shape[1]
    row = lax.broadcasted_iota(jnp.int32, (BLOCK, ROWS), 0).astype(jnp.float32)
    at = 0
    for n, ref in zip(shards, blocks):
        for i in range(n):
            for source in range(2):
                base = source * 2 * ROWS
                k[source, at : at + ROWS, :] = ref[i, base : base + ROWS]
                v[source, :HD, at : at + ROWS] = ref[i, base + ROWS : base + 2 * ROWS]
            ids = ref[i, 4 * ROWS : 4 * ROWS + POS_ROWS].astype(jnp.float32)
            for part in range(ROWS // BLOCK):
                key_pos = ids[0:1, part * BLOCK : part * BLOCK + 1] * BLOCK + row
                rows = slice(at + part * BLOCK, at + (part + 1) * BLOCK)
                cap[rows, :] = jnp.where(key_pos <= pos_ref[...], jnp.inf, MASKED)
            at += ROWS
    for source in range(2):
        v[source, HD:, :] = jnp.ones((POS_ROWS, count), jnp.bfloat16)

    def scores(j):
        q = jnp.concatenate([q_ref[j, :, h * HD : (h + 1) * HD] for h in range(HEADS)], axis=0)
        return lax.dot_general(
            k[warm_ref[j]], q, (((1,), (1,)), ((), ())), preferred_element_type=jnp.float32
        )

    def absorb(j, s):
        s = jnp.minimum(s, jnp.concatenate([cap[...]] * HEADS, axis=1))
        m = jnp.max(s, axis=0, keepdims=True)
        if not first:
            m_old = m_in[j, 0:1, :]
            m = jnp.maximum(m_old, m)
        w = jnp.exp2((s - m) * SCALE).astype(jnp.bfloat16)
        o = lax.dot_general(
            v[warm_ref[j]], w, (((1,), (0,)), ((), ())), preferred_element_type=jnp.float32
        )
        acc, den = o[:HD], o[HD : HD + 8]
        if not first:
            f = jnp.exp2((m_old - m) * SCALE)
            acc = acc + f * a_in[j]
            den = den + f * l_in[j]
        if last:
            done = acc / den[0:1]
            for h in range(HEADS):
                cols = slice(h * HD, (h + 1) * HD)
                outs[0][j, :, cols] = done[:, cols].T.astype(jnp.bfloat16)
        else:
            outs[0][j] = jnp.broadcast_to(m, den.shape)
            outs[1][j] = den
            outs[2][j] = acc

    @pl.loop(0, LAYERS // SLABS)
    def _(step):
        base = step * SLABS
        s = scores(base)
        for j in range(SLABS):
            ahead = scores(base + j + 1) if j + 1 < SLABS else None
            absorb(base + j, s)
            s = ahead


def attend(warm, q, pos, blocks, state, last):
    shards = tuple(b.shape[0] for b in blocks)
    count = sum(shards) * ROWS
    args = [warm, q, pos, *blocks]
    aliases = {}
    if state is not None:
        if not last:
            aliases = {len(args) + i: i for i in range(len(state))}
        args += list(state)
    whole = pl.BlockSpec(memory_space=pltpu.VMEM)
    one = jax.ShapeDtypeStruct((LAYERS, 8, WIDE), jnp.float32)
    acc = jax.ShapeDtypeStruct((LAYERS, HD, WIDE), jnp.float32)
    done = jax.ShapeDtypeStruct((LAYERS, ROWS, WIDE), jnp.bfloat16)
    return pl.pallas_call(
        functools.partial(attend_body, shards, state is None, last),
        in_specs=[pl.BlockSpec(memory_space=pltpu.SMEM)] + [whole] * (len(args) - 1),
        out_specs=whole if last else [whole] * 3,
        out_shape=done if last else [one, one, acc],
        scratch_shapes=[
            pltpu.VMEM((2, count, HD), jnp.bfloat16),
            pltpu.VMEM((2, HD + POS_ROWS, count), jnp.bfloat16),
            pltpu.VMEM((count, ROWS), jnp.float32),
        ],
        input_output_aliases=aliases,
        compiler_params=pltpu.CompilerParams(vmem_limit_bytes=24 << 20),
        cost_estimate=pl.CostEstimate(
            flops=4 * ROWS * H * count * HD,
            bytes_accessed=8 << 20,
            transcendentals=ROWS * H * count,
        ),
        name="attend",
    )(*args)


def turn(value, axis, size, shift):
    return lax.ppermute(value, axis, [(i, (i + shift) % size) for i in range(size)])


def pick(slabs, index):
    return lax.dynamic_index_in_dim(slabs, index, 0, keepdims=False)


def swap(slabs, index):
    other = turn(pick(slabs, index), "core", 2, 1)
    return lax.dynamic_update_index_in_dim(slabs, other, index, 0)


def per_device(sizes, queries, key_values, token_pos, layer_of_section):
    nz, nyh = sizes["z"], sizes["yh"]
    core = lax.axis_index("core")
    ids = jnp.arange(LAYERS, dtype=jnp.int32)
    holder = jnp.sum(jnp.where(layer_of_section[None, :] == ids[:, None], ids[None, :], 0), axis=1)
    warm, other_warm = pick(holder, core), pick(holder, 1 - core)
    kv = key_values[0].reshape(ROWS, 2, KVH, HD)
    heads = jnp.stack([kv[:, 0].transpose(1, 0, 2), kv[:, 1].transpose(1, 2, 0)], axis=1)
    pieces = jnp.broadcast_to(
        heads.reshape(KVH, 1, 2 * ROWS, HD), (KVH, LAYERS // KVH, 2 * ROWS, HD)
    ).reshape(LAYERS, 2 * ROWS, HD)
    pieces = lax.all_to_all(pieces, SECTION, 0, 0)
    block_ids = jnp.broadcast_to((token_pos // BLOCK).astype(jnp.bfloat16)[None, :], (POS_ROWS, ROWS))
    shard = jnp.concatenate([pick(pieces, holder[LAYERS - 1]), pick(pieces, warm), block_ids], axis=0)
    line = jnp.stack([shard] + [turn(shard, "yh", nyh, shift) for shift in range(1, nyh)])
    q = queries[0].reshape(ROWS, LAYERS, WIDE).transpose(1, 0, 2)
    q, line = lax.optimization_barrier((q, line))
    up, down = turn(line, "z", nz, 1), turn(line, "z", nz, -1)
    q = lax.all_to_all(q, SECTION, 0, 0)
    q = swap(q, other_warm)
    use_warm = ((ids == warm) | (ids == other_warm)).astype(jnp.int32)
    pos = token_pos.astype(jnp.float32)[None, :]

    def part(blocks, state, last=False):
        return attend(use_warm, q, pos, blocks, state, last)

    state = part([line], None)
    up, down, state = lax.optimization_barrier((up, down, state))
    held = [up, down]
    for _ in range(nz // 2 - 2):
        up, down = turn(up, "z", nz, 1), turn(down, "z", nz, -1)
        state = part(held, state)
        up, down, state = lax.optimization_barrier((up, down, state))
        held = [up, down]
    half = nyh // 2
    last_up, last_down = turn(up[:half], "z", nz, 1), turn(down[half:], "z", nz, -1)
    state = part(held, state)
    last_up, last_down, state = lax.optimization_barrier((last_up, last_down, state))
    out = swap(part([last_up, last_down], state, True), other_warm)
    out = lax.all_to_all(out, SECTION, 0, 0)
    return out.transpose(1, 0, 2).reshape(1, ROWS, H * HD)


def solution(mesh):
    sizes = {"x": 4, "yl": 2, "core": 2, "z": 8, "yh": 4}
    fine = Mesh(mesh.devices.reshape(tuple(sizes.values())), tuple(sizes))
    ctx = ("z", "yh")
    in_specs = (P(SECTION, ctx, None), P(SECTION, ctx, None, None), P(ctx), P())
    return jax.shard_map(
        functools.partial(per_device, sizes),
        mesh=fine,
        in_specs=in_specs,
        out_specs=P(SECTION, ctx, None),
        check_vma=False,
    )
```

```python
import functools

import jax
import jax.numpy as jnp
from jax import lax
from jax.experimental import pallas as pl
from jax.experimental.pallas import tpu as pltpu
from jax.sharding import Mesh, PartitionSpec as P

H = 32
KVH = 4
HD = 128
BLOCK = 64
WARM = 2
LAYERS = 16
ROWS = 128
HEADS = H // LAYERS
WIDE = HEADS * HD
SLABS = 8
POS_ROWS = 16
PART = 2 * ROWS
LINE_ROWS = 3 * PART + 2 * POS_ROWS
HANDED_ROWS = 2 * PART + POS_ROWS
MASKED = -1e30
SCALE = 1.4426950408889634 / HD**0.5
SECTION = ("x", "yl", "core")


def attend_body(shards, first, last, *refs):
    it = iter(refs)
    info, q_ref, pos_ref = next(it), next(it), next(it)
    blocks = [next(it) for _ in shards]
    if not first:
        m_in, l_in, a_in = next(it), next(it), next(it)
    outs = [next(it)] if last else [next(it), next(it), next(it)]
    k, v, cap = it
    count = k.shape[1]
    row = lax.broadcasted_iota(jnp.int32, (BLOCK, ROWS), 0).astype(jnp.float32)
    at = 0
    for n, ref in zip(shards, blocks):
        place = LAYERS + (0 if ref.shape[1] == LINE_ROWS else 3)
        starts = [pl.multiple_of(info[place + i], POS_ROWS) for i in range(3)]
        for i in range(n):
            for source in range(2):
                k[source, at : at + ROWS, :] = ref[i, pl.ds(starts[source], ROWS), :]
                v[source, :HD, at : at + ROWS] = ref[i, pl.ds(starts[source] + ROWS, ROWS), :]
            ids = ref[i, pl.ds(starts[2], POS_ROWS), :].astype(jnp.float32)
            for part in range(ROWS // BLOCK):
                key_pos = ids[0:1, part * BLOCK : part * BLOCK + 1] * BLOCK + row
                rows = slice(at + part * BLOCK, at + (part + 1) * BLOCK)
                cap[rows, :] = jnp.where(key_pos <= pos_ref[...], jnp.inf, MASKED)
            at += ROWS
    for source in range(2):
        v[source, HD:, :] = jnp.ones((POS_ROWS, count), jnp.bfloat16)

    def scores(j):
        q = jnp.concatenate([q_ref[j, :, h * HD : (h + 1) * HD] for h in range(HEADS)], axis=0)
        return lax.dot_general(
            k[info[j]], q, (((1,), (1,)), ((), ())), preferred_element_type=jnp.float32
        )

    def absorb(j, s):
        s = jnp.minimum(s, jnp.concatenate([cap[...]] * HEADS, axis=1))
        m = jnp.max(s, axis=0, keepdims=True)
        if not first:
            m_old = m_in[j, 0:1, :]
            m = jnp.maximum(m_old, m)
        w = jnp.exp2((s - m) * SCALE).astype(jnp.bfloat16)
        o = lax.dot_general(
            v[info[j]], w, (((1,), (0,)), ((), ())), preferred_element_type=jnp.float32
        )
        acc, den = o[:HD], o[HD : HD + 8]
        if not first:
            f = jnp.exp2((m_old - m) * SCALE)
            acc = acc + f * a_in[j]
            den = den + f * l_in[j]
        if last:
            done = acc / den[0:1]
            for h in range(HEADS):
                cols = slice(h * HD, (h + 1) * HD)
                outs[0][j, :, cols] = done[:, cols].T.astype(jnp.bfloat16)
        else:
            outs[0][j] = jnp.broadcast_to(m, den.shape)
            outs[1][j] = den
            outs[2][j] = acc

    @pl.loop(0, LAYERS // SLABS)
    def _(step):
        base = step * SLABS
        s = scores(base)
        for j in range(SLABS):
            ahead = scores(base + j + 1) if j + 1 < SLABS else None
            absorb(base + j, s)
            s = ahead


def attend(info, q, pos, blocks, state, last):
    shards = tuple(b.shape[0] for b in blocks)
    count = sum(shards) * ROWS
    args = [info, q, pos, *blocks]
    aliases = {}
    if state is not None:
        if not last:
            aliases = {len(args) + i: i for i in range(len(state))}
        args += list(state)
    whole = pl.BlockSpec(memory_space=pltpu.VMEM)
    one = jax.ShapeDtypeStruct((LAYERS, 8, WIDE), jnp.float32)
    acc = jax.ShapeDtypeStruct((LAYERS, HD, WIDE), jnp.float32)
    done = jax.ShapeDtypeStruct((LAYERS, ROWS, WIDE), jnp.bfloat16)
    return pl.pallas_call(
        functools.partial(attend_body, shards, state is None, last),
        in_specs=[pl.BlockSpec(memory_space=pltpu.SMEM)] + [whole] * (len(args) - 1),
        out_specs=whole if last else [whole] * 3,
        out_shape=done if last else [one, one, acc],
        scratch_shapes=[
            pltpu.VMEM((2, count, HD), jnp.bfloat16),
            pltpu.VMEM((2, HD + POS_ROWS, count), jnp.bfloat16),
            pltpu.VMEM((count, ROWS), jnp.float32),
        ],
        input_output_aliases=aliases,
        compiler_params=pltpu.CompilerParams(vmem_limit_bytes=24 << 20),
        cost_estimate=pl.CostEstimate(
            flops=4 * ROWS * H * count * HD,
            bytes_accessed=8 << 20,
            transcendentals=ROWS * H * count,
        ),
        name="attend",
    )(*args)


def turn(value, axis, size, shift):
    return lax.ppermute(value, axis, [(i, (i + shift) % size) for i in range(size)])


def packed(kv):
    def body(kv_ref, out_ref):
        for h in range(KVH):
            k = kv_ref[:, h * HD : (h + 1) * HD]
            v = kv_ref[:, (KVH + h) * HD : (KVH + h + 1) * HD].T
            for yl in range(LAYERS // KVH // 2):
                out_ref[h * 4 + yl * 2] = k
                out_ref[h * 4 + yl * 2 + 1] = v

    return pl.pallas_call(
        body,
        in_specs=[pl.BlockSpec(memory_space=pltpu.VMEM)],
        out_specs=pl.BlockSpec(memory_space=pltpu.VMEM),
        out_shape=jax.ShapeDtypeStruct((LAYERS, ROWS, HD), jnp.bfloat16),
        name="pack",
    )(kv)


def joined(core, mine, theirs):
    def body(core_ref, mine_ref, theirs_ref, out_ref):
        def fill(k_ref, v_ref):
            for i in range(mine.shape[0]):
                for s in range(3):
                    rows = slice(s * ROWS, (s + 1) * ROWS)
                    at = POS_ROWS + s * PART
                    out_ref[i, at : at + ROWS] = k_ref[i, rows]
                    out_ref[i, at + ROWS : at + PART] = v_ref[i, rows]

        for i in range(mine.shape[0]):
            out_ref[i, :POS_ROWS] = mine_ref[i, 3 * ROWS :]
            out_ref[i, LINE_ROWS - POS_ROWS :] = mine_ref[i, 3 * ROWS :]

        @pl.when(core_ref[0] == 0)
        def _():
            fill(mine_ref, theirs_ref)

        @pl.when(core_ref[0] != 0)
        def _():
            fill(theirs_ref, mine_ref)

    whole = pl.BlockSpec(memory_space=pltpu.VMEM)
    return pl.pallas_call(
        body,
        in_specs=[pl.BlockSpec(memory_space=pltpu.SMEM), whole, whole],
        out_specs=whole,
        out_shape=jax.ShapeDtypeStruct((mine.shape[0], LINE_ROWS, HD), jnp.bfloat16),
        name="join",
    )(core.astype(jnp.int32).reshape(1), mine, theirs)


def pick(slabs, index):
    return lax.dynamic_index_in_dim(slabs, index, 0, keepdims=False)


def swap(slabs, index):
    other = turn(pick(slabs, index), "core", 2, 1)
    return lax.dynamic_update_index_in_dim(slabs, other, index, 0)


def per_device(sizes, queries, key_values, token_pos, layer_of_section):
    nz, nyh = sizes["z"], sizes["yh"]
    core = lax.axis_index("core")
    ids = jnp.arange(LAYERS, dtype=jnp.int32)
    holder = jnp.sum(jnp.where(layer_of_section[None, :] == ids[:, None], ids[None, :], 0), axis=1)
    warm, other_warm = pick(holder, core), pick(holder, 1 - core)
    pieces = packed(key_values[0].reshape(ROWS, 2 * KVH * HD))
    pieces = lax.all_to_all(pieces, SECTION, 0, 0)
    block_ids = jnp.broadcast_to((token_pos // BLOCK).astype(jnp.bfloat16)[None, :], (POS_ROWS, ROWS))
    wanted = [holder[0], holder[LAYERS - 1], holder[1]]
    shard = jnp.concatenate([pick(pieces, index) for index in wanted] + [block_ids], axis=0)
    mine = jnp.stack([shard] + [turn(shard, "yh", nyh, shift) for shift in range(1, nyh)])
    theirs = turn(mine, "core", 2, 1)
    line = joined(core, mine, theirs)
    q, line = lax.optimization_barrier((queries[0], line))
    q = q.reshape(ROWS, LAYERS, WIDE).transpose(1, 0, 2)

    pairs = [(z, (z + 1) % nz) for z in range(nz)] + [(nz + z, nz + (z - 1) % nz) for z in range(nz)]

    def onward(value):
        return lax.ppermute(value, ("core", "z"), pairs)

    def handed(value):
        start = (1 - core) * (PART + POS_ROWS)
        return turn(lax.dynamic_slice_in_dim(value, start, HANDED_ROWS, axis=1), "core", 2, 1)

    arrived = onward(line)
    q = lax.all_to_all(q, SECTION, 0, 0)
    q = swap(q, other_warm)
    use_warm = ((ids == warm) | (ids == other_warm)).astype(jnp.int32)
    top_row = POS_ROWS + PART
    whole_rows = [top_row, POS_ROWS + 2 * PART * core, 0]
    handed_rows = [(1 - core) * top_row, (1 - core) * POS_ROWS + core * PART, core * 2 * PART]
    info = jnp.concatenate([use_warm, jnp.stack(whole_rows + handed_rows).astype(jnp.int32)])
    pos = token_pos.astype(jnp.float32)[None, :]

    def part(blocks, state, last=False):
        return attend(info, q, pos, blocks, state, last)

    held, state = [line], None
    half = nyh // 2
    for step in range(nz // 2 - 1):
        if step < nz // 2 - 2:
            coming = onward(arrived)
        else:
            coming = onward(lax.dynamic_slice_in_dim(arrived, core * half, half, axis=0))
        passed = handed(arrived)
        state = part(held, state)
        held = [arrived, passed]
        arrived, held, state = lax.optimization_barrier((coming, held, state))
    passed = handed(arrived)
    state = part(held, state)
    out = swap(part([arrived, passed], state, True), other_warm)
    out = lax.all_to_all(out, SECTION, 0, 0)
    return out.transpose(1, 0, 2).reshape(1, ROWS, H * HD)


def solution(mesh):
    sizes = {"x": 4, "yl": 2, "core": 2, "z": 8, "yh": 4}
    fine = Mesh(mesh.devices.reshape(tuple(sizes.values())), tuple(sizes))
    ctx = ("z", "yh")
    in_specs = (P(SECTION, ctx, None), P(SECTION, ctx, None, None), P(ctx), P())
    return jax.shard_map(
        functools.partial(per_device, sizes),
        mesh=fine,
        in_specs=in_specs,
        out_specs=P(SECTION, ctx, None),
        check_vma=False,
    )
```

```python
import functools

import jax
import jax.numpy as jnp
from jax import lax
from jax.experimental import pallas as pl
from jax.experimental.pallas import tpu as pltpu
from jax.sharding import Mesh, PartitionSpec as P

H = 32
KVH = 4
HD = 128
GROUP = H // KVH
BLOCK = 64
WARM = 2
LAYERS = 16
ROWS = 128
WIDE = 2 * HD
SLABS = GROUP * HD // WIDE
PART = 2 * ROWS
POS_ROWS = 16
RING = 3
MASKED = -1e30
SCALE = 1.4426950408889634 / HD**0.5
SECTION = ("x", "yl", "core")
VMEM = pl.BlockSpec(memory_space=pltpu.VMEM)


def attend_body(heads, offset, shards, first, last, extra, *refs):
    it = iter(refs)
    q_ref, pos_ref = next(it), next(it)
    blocks = [next(it) for _ in shards]
    if not first:
        m_in, l_in, a_in = next(it), next(it), next(it)
    if extra:
        extra_ref = next(it)
    outs = [next(it)] if last else [next(it), next(it), next(it)]
    k, v, cap = it
    count = k.shape[1]
    row = lax.broadcasted_iota(jnp.int32, (BLOCK, ROWS), 0).astype(jnp.float32)
    at = 0
    for n, ref in zip(shards, blocks):
        for i in range(n):
            for h in range(heads):
                base = h * PART
                k[h, at : at + ROWS, :] = ref[i, base : base + ROWS]
                v[h, :HD, at : at + ROWS] = ref[i, base + ROWS : base + PART]
            ids = ref[i, heads * PART :].astype(jnp.float32)
            for part in range(ROWS // BLOCK):
                key_pos = ids[0:1, part * BLOCK : part * BLOCK + 1] * BLOCK + row
                rows = slice(at + part * BLOCK, at + (part + 1) * BLOCK)
                cap[rows, :] = jnp.where(key_pos <= pos_ref[...], jnp.inf, MASKED)
            at += ROWS
    for h in range(heads):
        v[h, HD:, :] = jnp.ones((POS_ROWS, count), jnp.bfloat16)

    def scores(j):
        col = (offset * SLABS + j) * WIDE
        q = jnp.concatenate([q_ref[:, col : col + HD], q_ref[:, col + HD : col + WIDE]], axis=0)
        return lax.dot_general(
            k[j // SLABS], q, (((1,), (1,)), ((), ())), preferred_element_type=jnp.float32
        )

    def absorb(j, s):
        s = jnp.minimum(s, jnp.concatenate([cap[...]] * 2, axis=1))
        m = jnp.max(s, axis=0, keepdims=True)
        if not first:
            m_old = m_in[j, 0:1, :]
            m = jnp.maximum(m_old, m)
        w = jnp.exp2((s - m) * SCALE).astype(jnp.bfloat16)
        o = lax.dot_general(
            v[j // SLABS], w, (((1,), (0,)), ((), ())), preferred_element_type=jnp.float32
        )
        acc, den = o[:HD], o[HD : HD + 8]
        if not first:
            f = jnp.exp2((m_old - m) * SCALE)
            acc = acc + f * a_in[j]
            den = den + f * l_in[j]
        if last:
            done = acc / den[0:1]
            for h in range(2):
                cols = slice(j * WIDE + h * HD, j * WIDE + (h + 1) * HD)
                outs[0][:, cols] = done[:, h * HD : (h + 1) * HD].T.astype(jnp.bfloat16)
        else:
            outs[0][j] = jnp.broadcast_to(m, den.shape)
            outs[1][j] = den
            outs[2][j] = acc

    if extra:
        outs[0][:, heads * GROUP * HD :] = extra_ref[...]
    s = scores(0)
    for j in range(heads * SLABS):
        ahead = scores(j + 1) if j + 1 < heads * SLABS else None
        absorb(j, s)
        s = ahead


def attend(q, pos, heads, offset, blocks, state, last, extra=None):
    shards = tuple(b.shape[0] for b in blocks)
    count = sum(shards) * ROWS
    pairs = heads * SLABS
    args = [q, pos, *blocks]
    aliases = {}
    if state is not None:
        if not last:
            aliases = {len(args) + i: i for i in range(len(state))}
        args += list(state)
    if extra is not None:
        args.append(extra)
    one = jax.ShapeDtypeStruct((pairs, 8, WIDE), jnp.float32)
    acc = jax.ShapeDtypeStruct((pairs, HD, WIDE), jnp.float32)
    columns = pairs * WIDE + (0 if extra is None else extra.shape[1])
    done = jax.ShapeDtypeStruct((ROWS, columns), jnp.bfloat16)
    return pl.pallas_call(
        functools.partial(
            attend_body, heads, offset, shards, state is None, last, extra is not None
        ),
        in_specs=[VMEM] * len(args),
        out_specs=VMEM if last else [VMEM] * 3,
        out_shape=done if last else [one, one, acc],
        scratch_shapes=[
            pltpu.VMEM((heads, count, HD), jnp.bfloat16),
            pltpu.VMEM((heads, HD + POS_ROWS, count), jnp.bfloat16),
            pltpu.VMEM((count, ROWS), jnp.float32),
        ],
        input_output_aliases=aliases,
        compiler_params=pltpu.CompilerParams(vmem_limit_bytes=32 << 20),
        cost_estimate=pl.CostEstimate(
            flops=4 * ROWS * heads * GROUP * count * HD,
            bytes_accessed=8 << 20,
            transcendentals=ROWS * heads * GROUP * count,
        ),
        name="attend",
    )(*args)


def packed(kv):
    def body(kv_ref, out_ref):
        for h in range(KVH):
            at = h * PART
            out_ref[at : at + ROWS] = kv_ref[:, h * HD : (h + 1) * HD]
            out_ref[at + ROWS : at + PART] = kv_ref[:, (KVH + h) * HD : (KVH + h + 1) * HD].T

    return pl.pallas_call(
        body,
        in_specs=[VMEM],
        out_specs=VMEM,
        out_shape=jax.ShapeDtypeStruct((KVH * PART, HD), jnp.bfloat16),
        name="pack",
    )(kv)


def turn(value, axis, size, shift):
    return lax.ppermute(value, axis, [(i, (i + shift) % size) for i in range(size)])


def around(value, axis, size):
    return [turn(value, axis, size, shift) for shift in range(1, size)]


def per_device(sizes, queries, key_values, token_pos, layer_of_section):
    nz, nyh = sizes["z"], sizes["yh"]
    section = lax.axis_index(SECTION)
    ids = jnp.arange(LAYERS, dtype=jnp.int32)
    layer = jnp.sum(jnp.where(ids == section, layer_of_section, 0))
    top_section = jnp.sum(jnp.where(layer_of_section == LAYERS - 1, ids, 0))
    own = packed(key_values[0].reshape(ROWS, 2 * KVH * HD))
    pieces = own.reshape(LAYERS, KVH * PART // LAYERS, HD)
    piece = lax.dynamic_index_in_dim(lax.all_to_all(pieces, SECTION, 0, 0), top_section, 0, True)
    top = lax.all_to_all(jnp.broadcast_to(piece, pieces.shape), SECTION, 0, 0)
    rows = jnp.where(layer < WARM, own, top.reshape(own.shape))
    block_ids = jnp.broadcast_to((token_pos // BLOCK).astype(jnp.bfloat16)[None, :], (POS_ROWS, ROWS))
    shard = jnp.concatenate([rows[: RING * PART], block_ids], axis=0)
    beside = jnp.concatenate([rows[RING * PART :], block_ids], axis=0)
    q = queries[0]
    pos = token_pos.astype(jnp.float32)[None, :]

    def ring_part(blocks, state, last=False, extra=None):
        return attend(q, pos, RING, 0, blocks, state, last, extra)

    def side_part(blocks, state, last=False):
        return attend(q, pos, KVH - RING, RING, blocks, state, last)

    line = jnp.stack([shard] + around(shard, "yh", nyh))
    column = lax.all_to_all(jnp.broadcast_to(beside[None], (nz, *beside.shape)), "z", 0, 0)
    line, column = lax.optimization_barrier((line, column))
    half, side_half = nyh // 2, nz // 2
    up, down = turn(line, "z", nz, 1), turn(line, "z", nz, -1)
    side_up = turn(column, "yh", nyh, 1)
    state = ring_part([line], None)
    up, down, side_up, state = lax.optimization_barrier((up, down, side_up, state))

    held = [up, down]
    up, down = turn(up, "z", nz, 1), turn(down, "z", nz, -1)
    side_down = turn(column, "yh", nyh, -1)
    far_up = turn(side_up[:side_half], "yh", nyh, 1)
    state, side = ring_part(held, state), side_part([column, side_up], None)
    up, down, side_down, far_up, state, side = lax.optimization_barrier(
        (up, down, side_down, far_up, state, side)
    )

    held = [up, down]
    up, down = turn(up, "z", nz, 1), turn(down, "z", nz, -1)
    far_down = turn(side_down[side_half:], "yh", nyh, -1)
    state = ring_part(held, state)
    up, down, far_down, state = lax.optimization_barrier((up, down, far_down, state))

    last_up, last_down = turn(up[:half], "z", nz, 1), turn(down[half:], "z", nz, -1)
    state = ring_part([up, down], state)
    side_out = side_part([side_down, far_up, far_down], side, True)
    last_up, last_down, state, side_out = lax.optimization_barrier((last_up, last_down, state, side_out))
    out = ring_part([last_up, last_down], state, True, side_out)
    return out[None]


def solution(mesh):
    sizes = {"x": 4, "yl": 2, "core": 2, "z": 8, "yh": 4}
    fine = Mesh(mesh.devices.reshape(tuple(sizes.values())), tuple(sizes))
    ctx = ("z", "yh")
    in_specs = (P(SECTION, ctx, None), P(SECTION, ctx, None, None), P(ctx), P())
    return jax.shard_map(
        functools.partial(per_device, sizes),
        mesh=fine,
        in_specs=in_specs,
        out_specs=P(SECTION, ctx, None),
        check_vma=False,
    )
```

```python
import functools

import jax
import jax.numpy as jnp
from jax import lax
from jax.experimental import pallas as pl
from jax.experimental.pallas import tpu as pltpu
from jax.sharding import Mesh, PartitionSpec as P

H = 32
KVH = 4
HD = 128
BLOCK = 64
WARM = 2
LAYERS = 16
ROWS = 128
HEADS = H // LAYERS
WIDE = HEADS * HD
SLABS = 8
POS_ROWS = 16
PART = 2 * ROWS
LINE_ROWS = 2 * PART + POS_ROWS
MASKED = -1e30
SCALE = 1.4426950408889634 / HD**0.5
SECTION = ("x", "yl", "core")


def attend_body(shards, first, last, *refs):
    it = iter(refs)
    warm_ref, q_ref, pos_ref = next(it), next(it), next(it)
    blocks = [next(it) for _ in shards]
    if not first:
        m_in, l_in, a_in = next(it), next(it), next(it)
    outs = [next(it)] if last else [next(it), next(it), next(it)]
    k, v, cap = it
    count = k.shape[1]
    row = lax.broadcasted_iota(jnp.int32, (BLOCK, ROWS), 0).astype(jnp.float32)
    at = 0
    for n, ref in zip(shards, blocks):
        for i in range(n):
            for source in range(2):
                base = source * 2 * ROWS
                k[source, at : at + ROWS, :] = ref[i, base : base + ROWS]
                v[source, :HD, at : at + ROWS] = ref[i, base + ROWS : base + 2 * ROWS]
            ids = ref[i, 4 * ROWS : 4 * ROWS + POS_ROWS].astype(jnp.float32)
            for part in range(ROWS // BLOCK):
                key_pos = ids[0:1, part * BLOCK : part * BLOCK + 1] * BLOCK + row
                rows = slice(at + part * BLOCK, at + (part + 1) * BLOCK)
                cap[rows, :] = jnp.where(key_pos <= pos_ref[...], jnp.inf, MASKED)
            at += ROWS
    for source in range(2):
        v[source, HD:, :] = jnp.ones((POS_ROWS, count), jnp.bfloat16)

    def scores(j):
        q = jnp.concatenate([q_ref[j, :, h * HD : (h + 1) * HD] for h in range(HEADS)], axis=0)
        return lax.dot_general(
            k[warm_ref[j]], q, (((1,), (1,)), ((), ())), preferred_element_type=jnp.float32
        )

    def absorb(j, s):
        s = jnp.minimum(s, jnp.concatenate([cap[...]] * HEADS, axis=1))
        m = jnp.max(s, axis=0, keepdims=True)
        if not first:
            m_old = m_in[j, 0:1, :]
            m = jnp.maximum(m_old, m)
        w = jnp.exp2((s - m) * SCALE).astype(jnp.bfloat16)
        o = lax.dot_general(
            v[warm_ref[j]], w, (((1,), (0,)), ((), ())), preferred_element_type=jnp.float32
        )
        acc, den = o[:HD], o[HD : HD + 8]
        if not first:
            f = jnp.exp2((m_old - m) * SCALE)
            acc = acc + f * a_in[j]
            den = den + f * l_in[j]
        if last:
            done = acc / den[0:1]
            for h in range(HEADS):
                cols = slice(h * HD, (h + 1) * HD)
                outs[0][j, :, cols] = done[:, cols].T.astype(jnp.bfloat16)
        else:
            outs[0][j] = jnp.broadcast_to(m, den.shape)
            outs[1][j] = den
            outs[2][j] = acc

    @pl.loop(0, LAYERS // SLABS)
    def _(step):
        base = step * SLABS
        s = scores(base)
        for j in range(SLABS):
            ahead = scores(base + j + 1) if j + 1 < SLABS else None
            absorb(base + j, s)
            s = ahead


def attend(warm, q, pos, blocks, state, last):
    shards = tuple(b.shape[0] for b in blocks)
    count = sum(shards) * ROWS
    args = [warm, q, pos, *blocks]
    aliases = {}
    if state is not None:
        if not last:
            aliases = {len(args) + i: i for i in range(len(state))}
        args += list(state)
    whole = pl.BlockSpec(memory_space=pltpu.VMEM)
    one = jax.ShapeDtypeStruct((LAYERS, 8, WIDE), jnp.float32)
    acc = jax.ShapeDtypeStruct((LAYERS, HD, WIDE), jnp.float32)
    done = jax.ShapeDtypeStruct((LAYERS, ROWS, WIDE), jnp.bfloat16)
    return pl.pallas_call(
        functools.partial(attend_body, shards, state is None, last),
        in_specs=[pl.BlockSpec(memory_space=pltpu.SMEM)] + [whole] * (len(args) - 1),
        out_specs=whole if last else [whole] * 3,
        out_shape=done if last else [one, one, acc],
        scratch_shapes=[
            pltpu.VMEM((2, count, HD), jnp.bfloat16),
            pltpu.VMEM((2, HD + POS_ROWS, count), jnp.bfloat16),
            pltpu.VMEM((count, ROWS), jnp.float32),
        ],
        input_output_aliases=aliases,
        compiler_params=pltpu.CompilerParams(vmem_limit_bytes=24 << 20),
        cost_estimate=pl.CostEstimate(
            flops=4 * ROWS * H * count * HD,
            bytes_accessed=8 << 20,
            transcendentals=ROWS * H * count,
        ),
        name="attend",
    )(*args)


def turn(value, axis, size, shift):
    return lax.ppermute(value, axis, [(i, (i + shift) % size) for i in range(size)])


def packed(kv):
    def body(kv_ref, out_ref):
        for h in range(KVH):
            k = kv_ref[:, h * HD : (h + 1) * HD]
            v = kv_ref[:, (KVH + h) * HD : (KVH + h + 1) * HD].T
            for yl in range(LAYERS // KVH // 2):
                out_ref[h * 4 + yl * 2] = k
                out_ref[h * 4 + yl * 2 + 1] = v

    return pl.pallas_call(
        body,
        in_specs=[pl.BlockSpec(memory_space=pltpu.VMEM)],
        out_specs=pl.BlockSpec(memory_space=pltpu.VMEM),
        out_shape=jax.ShapeDtypeStruct((LAYERS, ROWS, HD), jnp.bfloat16),
        name="pack",
    )(kv)


def joined(core, mine, theirs):
    def body(core_ref, mine_ref, theirs_ref, out_ref):
        def fill(k_ref, v_ref):
            for i in range(mine.shape[0]):
                for s in range(2):
                    rows = slice(s * ROWS, (s + 1) * ROWS)
                    at = s * PART
                    out_ref[i, at : at + ROWS] = k_ref[i, rows]
                    out_ref[i, at + ROWS : at + PART] = v_ref[i, rows]

        for i in range(mine.shape[0]):
            out_ref[i, 2 * PART :] = mine_ref[i, 2 * ROWS :]

        @pl.when(core_ref[0] == 0)
        def _():
            fill(mine_ref, theirs_ref)

        @pl.when(core_ref[0] != 0)
        def _():
            fill(theirs_ref, mine_ref)

    whole = pl.BlockSpec(memory_space=pltpu.VMEM)
    return pl.pallas_call(
        body,
        in_specs=[pl.BlockSpec(memory_space=pltpu.SMEM), whole, whole],
        out_specs=whole,
        out_shape=jax.ShapeDtypeStruct((mine.shape[0], LINE_ROWS, HD), jnp.bfloat16),
        name="join",
    )(core.astype(jnp.int32).reshape(1), mine, theirs)


def pick(slabs, index):
    return lax.dynamic_index_in_dim(slabs, index, 0, keepdims=False)


def swap(slabs, index):
    other = turn(pick(slabs, index), "yl", 2, 1)
    return lax.dynamic_update_index_in_dim(slabs, other, index, 0)


def per_device(sizes, queries, key_values, token_pos, layer_of_section):
    nz, nyh = sizes["z"], sizes["yh"]
    core, yl = lax.axis_index("core"), lax.axis_index("yl")
    ids = jnp.arange(LAYERS, dtype=jnp.int32)
    holder = jnp.sum(jnp.where(layer_of_section[None, :] == ids[:, None], ids[None, :], 0), axis=1)
    warm, other_warm = pick(holder, yl), pick(holder, 1 - yl)
    pieces = packed(key_values[0].reshape(ROWS, 2 * KVH * HD))
    pieces = lax.all_to_all(pieces, SECTION, 0, 0)
    block_ids = jnp.broadcast_to((token_pos // BLOCK).astype(jnp.bfloat16)[None, :], (POS_ROWS, ROWS))
    wanted = [holder[LAYERS - 1], warm]
    shard = jnp.concatenate([pick(pieces, index) for index in wanted] + [block_ids], axis=0)
    mine = jnp.stack([shard] + [turn(shard, "yh", nyh, shift) for shift in range(1, nyh)])
    theirs = turn(mine, "core", 2, 1)
    line = joined(core, mine, theirs)
    q, line = lax.optimization_barrier((queries[0], line))
    q = q.reshape(ROWS, LAYERS, WIDE).transpose(1, 0, 2)

    pairs = [(z, (z + 1) % nz) for z in range(nz)] + [(nz + z, nz + (z - 1) % nz) for z in range(nz)]

    def onward(value):
        return lax.ppermute(value, ("core", "z"), pairs)

    def handed(value):
        return turn(value, "core", 2, 1)

    arrived = onward(line)
    q = lax.all_to_all(q, SECTION, 0, 0)
    q = swap(q, other_warm)
    use_warm = ((ids == warm) | (ids == other_warm)).astype(jnp.int32)
    pos = token_pos.astype(jnp.float32)[None, :]

    def part(blocks, state, last=False):
        return attend(use_warm, q, pos, blocks, state, last)

    held, state = [line], None
    half = nyh // 2
    for step in range(nz // 2 - 1):
        if step < nz // 2 - 2:
            coming = onward(arrived)
        else:
            coming = onward(lax.dynamic_slice_in_dim(arrived, core * half, half, axis=0))
        passed = handed(arrived)
        state = part(held, state)
        held = [arrived, passed]
        arrived, held, state = lax.optimization_barrier((coming, held, state))
    passed = handed(arrived)
    state = part(held, state)
    out = swap(part([arrived, passed], state, True), other_warm)
    out = lax.all_to_all(out, SECTION, 0, 0)
    return out.transpose(1, 0, 2).reshape(1, ROWS, H * HD)


def solution(mesh):
    sizes = {"x": 4, "yl": 2, "core": 2, "z": 8, "yh": 4}
    fine = Mesh(mesh.devices.reshape(tuple(sizes.values())), tuple(sizes))
    ctx = ("z", "yh")
    in_specs = (P(SECTION, ctx, None), P(SECTION, ctx, None, None), P(ctx), P())
    return jax.shard_map(
        functools.partial(per_device, sizes),
        mesh=fine,
        in_specs=in_specs,
        out_specs=P(SECTION, ctx, None),
        check_vma=False,
    )
```

```python
import functools

import jax
import jax.numpy as jnp
from jax import lax
from jax.experimental import pallas as pl
from jax.experimental.pallas import tpu as pltpu
from jax.sharding import Mesh, PartitionSpec as P

H = 32
KVH = 4
HD = 128
BLOCK = 64
WARM = 2
LAYERS = 16
ROWS = 128
HEADS = H // LAYERS
WIDE = HEADS * HD
SLABS = 8
POS_ROWS = 16
PART = 2 * ROWS
LINE_ROWS = 2 * PART + POS_ROWS
MASKED = -1e30
SCALE = 1.4426950408889634 / HD**0.5
SECTION = ("x", "yl", "core")


def attend_body(shards, first, last, *refs):
    it = iter(refs)
    warm_ref, q_ref, pos_ref = next(it), next(it), next(it)
    blocks = [next(it) for _ in shards]
    if not first:
        m_in, l_in, a_in = next(it), next(it), next(it)
    outs = [next(it)] if last else [next(it), next(it), next(it)]
    k, v, cap = it
    count = k.shape[1]
    row = lax.broadcasted_iota(jnp.int32, (BLOCK, ROWS), 0).astype(jnp.float32)
    at = 0
    for n, ref in zip(shards, blocks):
        for i in range(n):
            for source in range(2):
                base = source * 2 * ROWS
                k[source, at : at + ROWS, :] = ref[i, base : base + ROWS]
                v[source, :HD, at : at + ROWS] = ref[i, base + ROWS : base + 2 * ROWS]
            ids = ref[i, 4 * ROWS : 4 * ROWS + POS_ROWS].astype(jnp.float32)
            for part in range(ROWS // BLOCK):
                key_pos = ids[0:1, part * BLOCK : part * BLOCK + 1] * BLOCK + row
                rows = slice(at + part * BLOCK, at + (part + 1) * BLOCK)
                cap[rows, :] = jnp.where(key_pos <= pos_ref[...], jnp.inf, MASKED)
            at += ROWS
    for source in range(2):
        v[source, HD:, :] = jnp.ones((POS_ROWS, count), jnp.bfloat16)

    def scores(j):
        q = jnp.concatenate([q_ref[j, :, h * HD : (h + 1) * HD] for h in range(HEADS)], axis=0)
        return lax.dot_general(
            k[warm_ref[j]], q, (((1,), (1,)), ((), ())), preferred_element_type=jnp.float32
        )

    def absorb(j, s):
        s = jnp.minimum(s, jnp.concatenate([cap[...]] * HEADS, axis=1))
        m = jnp.max(s, axis=0, keepdims=True)
        if not first:
            m_old = m_in[j, 0:1, :]
            m = jnp.maximum(m_old, m)
        w = jnp.exp2((s - m) * SCALE).astype(jnp.bfloat16)
        o = lax.dot_general(
            v[warm_ref[j]], w, (((1,), (0,)), ((), ())), preferred_element_type=jnp.float32
        )
        acc, den = o[:HD], o[HD : HD + 8]
        if not first:
            f = jnp.exp2((m_old - m) * SCALE)
            acc = acc + f * a_in[j]
            den = den + f * l_in[j]
        if last:
            done = acc / den[0:1]
            for h in range(HEADS):
                cols = slice(h * HD, (h + 1) * HD)
                outs[0][j, :, cols] = done[:, cols].T.astype(jnp.bfloat16)
        else:
            outs[0][j] = jnp.broadcast_to(m, den.shape)
            outs[1][j] = den
            outs[2][j] = acc

    @pl.loop(0, LAYERS // SLABS)
    def _(step):
        base = step * SLABS
        s = scores(base)
        for j in range(SLABS):
            ahead = scores(base + j + 1) if j + 1 < SLABS else None
            absorb(base + j, s)
            s = ahead


def attend(warm, q, pos, blocks, state, last):
    shards = tuple(b.shape[0] for b in blocks)
    count = sum(shards) * ROWS
    args = [warm, q, pos, *blocks]
    aliases = {}
    if state is not None:
        if not last:
            aliases = {len(args) + i: i for i in range(len(state))}
        args += list(state)
    whole = pl.BlockSpec(memory_space=pltpu.VMEM)
    one = jax.ShapeDtypeStruct((LAYERS, 8, WIDE), jnp.float32)
    acc = jax.ShapeDtypeStruct((LAYERS, HD, WIDE), jnp.float32)
    done = jax.ShapeDtypeStruct((LAYERS, ROWS, WIDE), jnp.bfloat16)
    return pl.pallas_call(
        functools.partial(attend_body, shards, state is None, last),
        in_specs=[pl.BlockSpec(memory_space=pltpu.SMEM)] + [whole] * (len(args) - 1),
        out_specs=whole if last else [whole] * 3,
        out_shape=done if last else [one, one, acc],
        scratch_shapes=[
            pltpu.VMEM((2, count, HD), jnp.bfloat16),
            pltpu.VMEM((2, HD + POS_ROWS, count), jnp.bfloat16),
            pltpu.VMEM((count, ROWS), jnp.float32),
        ],
        input_output_aliases=aliases,
        compiler_params=pltpu.CompilerParams(vmem_limit_bytes=24 << 20),
        cost_estimate=pl.CostEstimate(
            flops=4 * ROWS * H * count * HD,
            bytes_accessed=8 << 20,
            transcendentals=ROWS * H * count,
        ),
        name="attend",
    )(*args)


def turn(value, axis, size, shift):
    return lax.ppermute(value, axis, [(i, (i + shift) % size) for i in range(size)])


def packed(kv):
    def body(kv_ref, out_ref):
        for h in range(KVH):
            k = kv_ref[:, h * HD : (h + 1) * HD]
            v = kv_ref[:, (KVH + h) * HD : (KVH + h + 1) * HD].T
            for yl in range(LAYERS // KVH // 2):
                out_ref[h * 4 + yl * 2] = k
                out_ref[h * 4 + yl * 2 + 1] = v

    return pl.pallas_call(
        body,
        in_specs=[pl.BlockSpec(memory_space=pltpu.VMEM)],
        out_specs=pl.BlockSpec(memory_space=pltpu.VMEM),
        out_shape=jax.ShapeDtypeStruct((LAYERS, ROWS, HD), jnp.bfloat16),
        name="pack",
    )(kv)


def joined(core, mine, theirs):
    def body(core_ref, mine_ref, theirs_ref, out_ref):
        def fill(k_ref, v_ref):
            for i in range(mine.shape[0]):
                for s in range(2):
                    rows = slice(s * ROWS, (s + 1) * ROWS)
                    at = s * PART
                    out_ref[i, at : at + ROWS] = k_ref[i, rows]
                    out_ref[i, at + ROWS : at + PART] = v_ref[i, rows]

        for i in range(mine.shape[0]):
            out_ref[i, 2 * PART :] = mine_ref[i, 2 * ROWS :]

        @pl.when(core_ref[0] == 0)
        def _():
            fill(mine_ref, theirs_ref)

        @pl.when(core_ref[0] != 0)
        def _():
            fill(theirs_ref, mine_ref)

    whole = pl.BlockSpec(memory_space=pltpu.VMEM)
    return pl.pallas_call(
        body,
        in_specs=[pl.BlockSpec(memory_space=pltpu.SMEM), whole, whole],
        out_specs=whole,
        out_shape=jax.ShapeDtypeStruct((mine.shape[0], LINE_ROWS, HD), jnp.bfloat16),
        name="join",
    )(core.astype(jnp.int32).reshape(1), mine, theirs)


def pick(slabs, index):
    return lax.dynamic_index_in_dim(slabs, index, 0, keepdims=False)


def swap(slabs, index):
    other = turn(pick(slabs, index), "yl", 2, 1)
    return lax.dynamic_update_index_in_dim(slabs, other, index, 0)


def per_device(sizes, queries, key_values, token_pos, layer_of_section):
    nz, nyh = sizes["z"], sizes["yh"]
    core, yl = lax.axis_index("core"), lax.axis_index("yl")
    ids = jnp.arange(LAYERS, dtype=jnp.int32)
    holder = jnp.sum(jnp.where(layer_of_section[None, :] == ids[:, None], ids[None, :], 0), axis=1)
    warm, other_warm = pick(holder, yl), pick(holder, 1 - yl)
    pieces = packed(key_values[0].reshape(ROWS, 2 * KVH * HD))
    pieces = lax.all_to_all(pieces, SECTION, 0, 0)
    q = queries[0].reshape(ROWS, LAYERS, WIDE).transpose(1, 0, 2)
    q, pieces = lax.optimization_barrier((q, pieces))
    q = lax.all_to_all(q, SECTION, 0, 0)
    q = swap(q, other_warm)
    use_warm = ((ids == warm) | (ids == other_warm)).astype(jnp.int32)
    pos = token_pos.astype(jnp.float32)[None, :]
    block_ids = jnp.broadcast_to((token_pos // BLOCK).astype(jnp.bfloat16)[None, :], (POS_ROWS, ROWS))
    wanted = [holder[LAYERS - 1], warm]
    shard = jnp.concatenate([pick(pieces, index) for index in wanted] + [block_ids], axis=0)
    mine = jnp.stack([shard] + [turn(shard, "yh", nyh, shift) for shift in range(1, nyh)])
    theirs = turn(mine, "core", 2, 1)
    line = joined(core, mine, theirs)

    pairs = [(z, (z + 1) % nz) for z in range(nz)] + [(nz + z, nz + (z - 1) % nz) for z in range(nz)]

    def onward(value):
        return lax.ppermute(value, ("core", "z"), pairs)

    def handed(value):
        return turn(value, "core", 2, 1)

    arrived = onward(line)

    def part(blocks, state, last=False):
        return attend(use_warm, q, pos, blocks, state, last)

    state = part([line], None)
    arrived, state = lax.optimization_barrier((arrived, state))
    half = nyh // 2
    for step in range(nz // 2 - 1):
        if step < nz // 2 - 2:
            coming = onward(arrived)
        else:
            coming = onward(lax.dynamic_slice_in_dim(arrived, core * half, half, axis=0))
        state = part([arrived, handed(arrived)], state)
        arrived, state = lax.optimization_barrier((coming, state))
    out = swap(part([arrived, handed(arrived)], state, True), other_warm)
    out = lax.all_to_all(out, SECTION, 0, 0)
    return out.transpose(1, 0, 2).reshape(1, ROWS, H * HD)


def solution(mesh):
    sizes = {"x": 4, "yl": 2, "core": 2, "z": 8, "yh": 4}
    fine = Mesh(mesh.devices.reshape(tuple(sizes.values())), tuple(sizes))
    ctx = ("z", "yh")
    in_specs = (P(SECTION, ctx, None), P(SECTION, ctx, None, None), P(ctx), P())
    return jax.shard_map(
        functools.partial(per_device, sizes),
        mesh=fine,
        in_specs=in_specs,
        out_specs=P(SECTION, ctx, None),
        check_vma=False,
    )
```

```python
import functools

import jax
import jax.numpy as jnp
from jax import lax
from jax.experimental import pallas as pl
from jax.experimental.pallas import tpu as pltpu
from jax.sharding import Mesh, PartitionSpec as P

H = 32
KVH = 4
HD = 128
BLOCK = 64
WARM = 2
LAYERS = 16
ROWS = 128
HEADS = H // LAYERS
WIDE = HEADS * HD
SLABS = 8
POS_ROWS = 16
HALF_ROWS = 2 * ROWS + POS_ROWS
MASKED = -1e30
SCALE = 1.4426950408889634 / HD**0.5
SECTION = ("x", "yl", "core")


def attend_body(shards, first, last, *refs):
    it = iter(refs)
    warm_ref, q_ref, pos_ref = next(it), next(it), next(it)
    blocks = [next(it) for _ in shards]
    if not first:
        m_in, l_in, a_in = next(it), next(it), next(it)
    outs = [next(it)] if last else [next(it), next(it), next(it)]
    k, v, cap = it
    count = k.shape[1]
    row = lax.broadcasted_iota(jnp.int32, (BLOCK, ROWS), 0).astype(jnp.float32)
    at = 0
    for n, ref in zip(shards, blocks):
        for i in range(n):
            for source in range(2):
                base = source * ROWS
                k[source, at : at + ROWS, :] = ref[i, base : base + ROWS]
                v[source, :HD, at : at + ROWS] = ref[i, HALF_ROWS + base : HALF_ROWS + base + ROWS]
            ids = ref[i, 2 * ROWS : HALF_ROWS].astype(jnp.float32)
            for part in range(ROWS // BLOCK):
                key_pos = ids[0:1, part * BLOCK : part * BLOCK + 1] * BLOCK + row
                rows = slice(at + part * BLOCK, at + (part + 1) * BLOCK)
                cap[rows, :] = jnp.where(key_pos <= pos_ref[...], jnp.inf, MASKED)
            at += ROWS
    for source in range(2):
        v[source, HD:, :] = jnp.ones((POS_ROWS, count), jnp.bfloat16)

    def scores(j):
        q = jnp.concatenate([q_ref[j, :, h * HD : (h + 1) * HD] for h in range(HEADS)], axis=0)
        return lax.dot_general(
            k[warm_ref[j]], q, (((1,), (1,)), ((), ())), preferred_element_type=jnp.float32
        )

    def absorb(j, s):
        s = jnp.minimum(s, jnp.concatenate([cap[...]] * HEADS, axis=1))
        m = jnp.max(s, axis=0, keepdims=True)
        if not first:
            m_old = m_in[j, 0:1, :]
            m = jnp.maximum(m_old, m)
        w = jnp.exp2((s - m) * SCALE).astype(jnp.bfloat16)
        o = lax.dot_general(
            v[warm_ref[j]], w, (((1,), (0,)), ((), ())), preferred_element_type=jnp.float32
        )
        acc, den = o[:HD], o[HD : HD + 8]
        if not first:
            f = jnp.exp2((m_old - m) * SCALE)
            acc = acc + f * a_in[j]
            den = den + f * l_in[j]
        if last:
            done = acc / den[0:1]
            for h in range(HEADS):
                cols = slice(h * HD, (h + 1) * HD)
                outs[0][j, :, cols] = done[:, cols].T.astype(jnp.bfloat16)
        else:
            outs[0][j] = jnp.broadcast_to(m, den.shape)
            outs[1][j] = den
            outs[2][j] = acc

    slabs = min(SLABS, q_ref.shape[0])

    @pl.loop(0, q_ref.shape[0] // slabs)
    def _(step):
        base = step * slabs
        s = scores(base)
        for j in range(slabs):
            ahead = scores(base + j + 1) if j + 1 < slabs else None
            absorb(base + j, s)
            s = ahead


def attend(warm, q, pos, blocks, state, last):
    shards = tuple(b.shape[0] for b in blocks)
    count = sum(shards) * ROWS
    layers = q.shape[0]
    args = [warm, q, pos, *blocks]
    aliases = {}
    if state is not None:
        if not last:
            aliases = {len(args) + i: i for i in range(len(state))}
        args += list(state)
    whole = pl.BlockSpec(memory_space=pltpu.VMEM)
    one = jax.ShapeDtypeStruct((layers, 8, WIDE), jnp.float32)
    acc = jax.ShapeDtypeStruct((layers, HD, WIDE), jnp.float32)
    done = jax.ShapeDtypeStruct((layers, ROWS, WIDE), jnp.bfloat16)
    return pl.pallas_call(
        functools.partial(attend_body, shards, state is None, last),
        in_specs=[pl.BlockSpec(memory_space=pltpu.SMEM)] + [whole] * (len(args) - 1),
        out_specs=whole if last else [whole] * 3,
        out_shape=done if last else [one, one, acc],
        scratch_shapes=[
            pltpu.VMEM((2, count, HD), jnp.bfloat16),
            pltpu.VMEM((2, HD + POS_ROWS, count), jnp.bfloat16),
            pltpu.VMEM((count, ROWS), jnp.float32),
        ],
        input_output_aliases=aliases,
        compiler_params=pltpu.CompilerParams(vmem_limit_bytes=24 << 20),
        cost_estimate=pl.CostEstimate(
            flops=4 * ROWS * layers * HEADS * count * HD,
            bytes_accessed=8 << 20,
            transcendentals=ROWS * layers * HEADS * count,
        ),
        name="attend",
    )(*args)


def turn(value, axis, size, shift):
    return lax.ppermute(value, axis, [(i, (i + shift) % size) for i in range(size)])


def packed(kv):
    def body(kv_ref, out_ref):
        for h in range(KVH):
            k = kv_ref[:, h * HD : (h + 1) * HD]
            v = kv_ref[:, (KVH + h) * HD : (KVH + h + 1) * HD].T
            for yl in range(LAYERS // KVH // 2):
                out_ref[h * 4 + yl * 2] = k
                out_ref[h * 4 + yl * 2 + 1] = v

    return pl.pallas_call(
        body,
        in_specs=[pl.BlockSpec(memory_space=pltpu.VMEM)],
        out_specs=pl.BlockSpec(memory_space=pltpu.VMEM),
        out_shape=jax.ShapeDtypeStruct((LAYERS, ROWS, HD), jnp.bfloat16),
        name="pack",
    )(kv)


def spread_columns(slabs):
    group = 4

    def body(in_ref, out_ref):
        for i in range(group):
            out_ref[:, i * WIDE : (i + 1) * WIDE] = in_ref[pl.program_id(0) * group + i]

    return pl.pallas_call(
        body,
        grid=(LAYERS // group,),
        in_specs=[pl.BlockSpec(memory_space=pltpu.VMEM)],
        out_specs=pl.BlockSpec((ROWS, group * WIDE), lambda i: (0, i)),
        out_shape=jax.ShapeDtypeStruct((ROWS, LAYERS * WIDE), slabs.dtype),
        name="columns",
    )(slabs)


def pick(slabs, index):
    return lax.dynamic_index_in_dim(slabs, index.astype(jnp.uint32), 0, keepdims=False)


def put(slabs, slab, index):
    return lax.dynamic_update_index_in_dim(slabs, slab, index.astype(jnp.uint32), 0)


def per_device(sizes, queries, key_values, token_pos, layer_of_section):
    nz, nyh = sizes["z"], sizes["yh"]
    core, yl = lax.axis_index("core"), lax.axis_index("yl")
    ids = jnp.arange(LAYERS, dtype=jnp.int32)
    holder = jnp.sum(jnp.where(layer_of_section[None, :] == ids[:, None], ids[None, :], 0), axis=1)
    top_holder = holder[LAYERS - 1]
    warm, other_warm = jnp.where(yl == 0, holder[0], holder[1]), jnp.where(yl == 0, holder[1], holder[0])
    use_warm = ((ids == warm) | (ids == other_warm)).astype(jnp.int32)
    pos = token_pos.astype(jnp.float32)[None, :]
    block_ids = jnp.broadcast_to((token_pos // BLOCK).astype(jnp.bfloat16)[None, :], (POS_ROWS, ROWS))
    pieces = packed(key_values[0].reshape(ROWS, 2 * KVH * HD))
    pieces = lax.all_to_all(pieces, SECTION, 0, 0)
    q = queries[0].reshape(ROWS, LAYERS, WIDE).transpose(1, 0, 2)
    q, pieces, top_holder, warm, other_warm, use_warm, pos, block_ids = lax.optimization_barrier(
        (q, pieces, top_holder, warm, other_warm, use_warm, pos, block_ids)
    )
    q = lax.all_to_all(q, SECTION, 0, 0)
    q_other = turn(pick(q, other_warm), "yl", 2, 1)
    q = put(q, q_other, other_warm)
    shard = jnp.concatenate([pick(pieces, top_holder), pick(pieces, warm), block_ids], axis=0)
    mine = jnp.stack([shard] + [turn(shard, "yh", nyh, shift) for shift in range(1, nyh)])
    theirs = turn(mine, "core", 2, 1)
    keys, values = jnp.where(core == 0, mine, theirs), jnp.where(core == 0, theirs, mine)
    line = jnp.concatenate([keys, values], axis=1)

    pairs = [(z, (z + 1) % nz) for z in range(nz)] + [(nz + z, nz + (z - 1) % nz) for z in range(nz)]

    def onward(value):
        return lax.ppermute(value, ("core", "z"), pairs)

    def handed(value):
        return turn(value, "core", 2, 1)

    arrived = onward(line)

    def part(blocks, state, last=False):
        return attend(use_warm, q, pos, blocks, state, last)

    state = part([line], None)
    arrived, state = lax.optimization_barrier((arrived, state))
    half = nyh // 2
    for step in range(nz // 2 - 1):
        if step < nz // 2 - 2:
            coming = onward(arrived)
        else:
            coming = onward(lax.dynamic_slice_in_dim(arrived, (core * half).astype(jnp.uint32), half, axis=0))
        state = part([arrived, handed(arrived)], state)
        arrived, state = lax.optimization_barrier((coming, state))
    held = [arrived, handed(arrived)]
    slab_state = [pick(value, other_warm)[None] for value in state]
    slab = attend(jnp.ones(1, jnp.int32), q_other[None], pos, held, slab_state, True)
    slab, state = lax.optimization_barrier((slab, state))
    back = turn(slab[0], "yl", 2, 1)
    out = put(part(held, state, True), back, other_warm)
    out = lax.all_to_all(out, SECTION, 0, 0)
    return spread_columns(out)[None]


def solution(mesh):
    sizes = {"x": 4, "yl": 2, "core": 2, "z": 8, "yh": 4}
    fine = Mesh(mesh.devices.reshape(tuple(sizes.values())), tuple(sizes))
    ctx = ("z", "yh")
    in_specs = (P(SECTION, ctx, None), P(SECTION, ctx, None, None), P(ctx), P())
    return jax.shard_map(
        functools.partial(per_device, sizes),
        mesh=fine,
        in_specs=in_specs,
        out_specs=P(SECTION, ctx, None),
        check_vma=False,
    )
```

```python
import functools

import jax
import jax.numpy as jnp
from jax import lax
from jax.experimental import pallas as pl
from jax.experimental.pallas import tpu as pltpu
from jax.sharding import Mesh, PartitionSpec as P

H = 32
KVH = 4
HD = 128
BLOCK = 64
WARM = 2
LAYERS = 16
ROWS = 128
HEADS = H // LAYERS
WIDE = HEADS * HD
SLABS = 8
POS_ROWS = 16
HALF_ROWS = 2 * ROWS + POS_ROWS
MASKED = -1e30
SCALE = 1.4426950408889634 / HD**0.5
SECTION = ("x", "yl", "core")


def attend_body(shards, first, last, *refs):
    it = iter(refs)
    warm_ref, q_ref, pos_ref = next(it), next(it), next(it)
    blocks = [next(it) for _ in shards]
    if not first:
        m_in, l_in, a_in = next(it), next(it), next(it)
    outs = [next(it)] if last else [next(it), next(it), next(it)]
    k, v, cap = it
    count = k.shape[1]
    row = lax.broadcasted_iota(jnp.int32, (BLOCK, ROWS), 0).astype(jnp.float32)
    at = 0
    for n, ref in zip(shards, blocks):
        for i in range(n):
            for source in range(2):
                base = source * ROWS
                k[source, at : at + ROWS, :] = ref[i, base : base + ROWS]
                v[source, :HD, at : at + ROWS] = ref[i, HALF_ROWS + base : HALF_ROWS + base + ROWS]
            ids = ref[i, 2 * ROWS : HALF_ROWS].astype(jnp.float32)
            for part in range(ROWS // BLOCK):
                key_pos = ids[0:1, part * BLOCK : part * BLOCK + 1] * BLOCK + row
                rows = slice(at + part * BLOCK, at + (part + 1) * BLOCK)
                cap[rows, :] = jnp.where(key_pos <= pos_ref[...], jnp.inf, MASKED)
            at += ROWS
    for source in range(2):
        v[source, HD:, :] = jnp.ones((POS_ROWS, count), jnp.bfloat16)

    def scores(j):
        q = jnp.concatenate([q_ref[j, :, h * HD : (h + 1) * HD] for h in range(HEADS)], axis=0)
        return lax.dot_general(
            k[warm_ref[j]], q, (((1,), (1,)), ((), ())), preferred_element_type=jnp.float32
        )

    def absorb(j, s):
        s = jnp.minimum(s, jnp.concatenate([cap[...]] * HEADS, axis=1))
        m = jnp.max(s, axis=0, keepdims=True)
        if not first:
            m_old = m_in[j, 0:1, :]
            m = jnp.maximum(m_old, m)
        w = jnp.exp2((s - m) * SCALE).astype(jnp.bfloat16)
        o = lax.dot_general(
            v[warm_ref[j]], w, (((1,), (0,)), ((), ())), preferred_element_type=jnp.float32
        )
        acc, den = o[:HD], o[HD : HD + 8]
        if not first:
            f = jnp.exp2((m_old - m) * SCALE)
            acc = acc + f * a_in[j]
            den = den + f * l_in[j]
        if last:
            done = acc / den[0:1]
            for h in range(HEADS):
                cols = slice(h * HD, (h + 1) * HD)
                outs[0][j, :, cols] = done[:, cols].T.astype(jnp.bfloat16)
        else:
            outs[0][j] = jnp.broadcast_to(m, den.shape)
            outs[1][j] = den
            outs[2][j] = acc

    slabs = min(SLABS, q_ref.shape[0])

    @pl.loop(0, q_ref.shape[0] // slabs)
    def _(step):
        base = step * slabs
        s = scores(base)
        for j in range(slabs):
            ahead = scores(base + j + 1) if j + 1 < slabs else None
            absorb(base + j, s)
            s = ahead


def attend(warm, q, pos, blocks, state, last):
    shards = tuple(b.shape[0] for b in blocks)
    count = sum(shards) * ROWS
    layers = q.shape[0]
    args = [warm, q, pos, *blocks]
    aliases = {}
    if state is not None:
        if not last:
            aliases = {len(args) + i: i for i in range(len(state))}
        args += list(state)
    whole = pl.BlockSpec(memory_space=pltpu.VMEM)
    one = jax.ShapeDtypeStruct((layers, 8, WIDE), jnp.float32)
    acc = jax.ShapeDtypeStruct((layers, HD, WIDE), jnp.float32)
    done = jax.ShapeDtypeStruct((layers, ROWS, WIDE), jnp.bfloat16)
    return pl.pallas_call(
        functools.partial(attend_body, shards, state is None, last),
        in_specs=[pl.BlockSpec(memory_space=pltpu.SMEM)] + [whole] * (len(args) - 1),
        out_specs=whole if last else [whole] * 3,
        out_shape=done if last else [one, one, acc],
        scratch_shapes=[
            pltpu.VMEM((2, count, HD), jnp.bfloat16),
            pltpu.VMEM((2, HD + POS_ROWS, count), jnp.bfloat16),
            pltpu.VMEM((count, ROWS), jnp.float32),
        ],
        input_output_aliases=aliases,
        compiler_params=pltpu.CompilerParams(vmem_limit_bytes=24 << 20),
        cost_estimate=pl.CostEstimate(
            flops=4 * ROWS * layers * HEADS * count * HD,
            bytes_accessed=8 << 20,
            transcendentals=ROWS * layers * HEADS * count,
        ),
        name="attend",
    )(*args)


def turn(value, axis, size, shift):
    return lax.ppermute(value, axis, [(i, (i + shift) % size) for i in range(size)])


def packed(kv):
    def body(kv_ref, out_ref):
        for h in range(KVH):
            k = kv_ref[:, h * HD : (h + 1) * HD]
            v = kv_ref[:, (KVH + h) * HD : (KVH + h + 1) * HD].T
            for yl in range(LAYERS // KVH // 2):
                out_ref[h * 4 + yl * 2] = k
                out_ref[h * 4 + yl * 2 + 1] = v

    return pl.pallas_call(
        body,
        in_specs=[pl.BlockSpec(memory_space=pltpu.VMEM)],
        out_specs=pl.BlockSpec(memory_space=pltpu.VMEM),
        out_shape=jax.ShapeDtypeStruct((LAYERS, ROWS, HD), jnp.bfloat16),
        name="pack",
    )(kv)


def pick(slabs, index):
    return lax.dynamic_index_in_dim(slabs, index.astype(jnp.uint32), 0, keepdims=False)


def put(slabs, slab, index):
    return lax.dynamic_update_index_in_dim(slabs, slab, index.astype(jnp.uint32), 0)


def per_device(sizes, queries, key_values, token_pos, layer_of_section):
    nz, nyh = sizes["z"], sizes["yh"]
    core, yl = lax.axis_index("core"), lax.axis_index("yl")
    ids = jnp.arange(LAYERS, dtype=jnp.int32)
    holder = jnp.sum(jnp.where(layer_of_section[None, :] == ids[:, None], ids[None, :], 0), axis=1)
    top_holder = holder[LAYERS - 1]
    warm, other_warm = jnp.where(yl == 0, holder[0], holder[1]), jnp.where(yl == 0, holder[1], holder[0])
    use_warm = ((ids == warm) | (ids == other_warm)).astype(jnp.int32)
    pos = token_pos.astype(jnp.float32)[None, :]
    block_ids = jnp.broadcast_to((token_pos // BLOCK).astype(jnp.bfloat16)[None, :], (POS_ROWS, ROWS))
    pieces = packed(key_values[0].reshape(ROWS, 2 * KVH * HD))
    pieces = lax.all_to_all(pieces, SECTION, 0, 0)
    q = queries[0].reshape(ROWS, LAYERS, WIDE).transpose(1, 0, 2)
    q, pieces, top_holder, warm, other_warm, use_warm, pos, block_ids = lax.optimization_barrier(
        (q, pieces, top_holder, warm, other_warm, use_warm, pos, block_ids)
    )
    shard = jnp.concatenate([pick(pieces, top_holder), pick(pieces, warm), block_ids], axis=0)
    mine = jnp.stack([shard] + [turn(shard, "yh", nyh, shift) for shift in range(1, nyh)])
    q, mine = lax.optimization_barrier((q, mine))
    q = lax.all_to_all(q, SECTION, 0, 0)
    q_other = turn(pick(q, other_warm), "yl", 2, 1)
    q = put(q, q_other, other_warm)
    theirs = turn(mine, "core", 2, 1)
    keys, values = jnp.where(core == 0, mine, theirs), jnp.where(core == 0, theirs, mine)
    line = jnp.concatenate([keys, values], axis=1)

    pairs = [(z, (z + 1) % nz) for z in range(nz)] + [(nz + z, nz + (z - 1) % nz) for z in range(nz)]

    def onward(value):
        return lax.ppermute(value, ("core", "z"), pairs)

    def handed(value):
        return turn(value, "core", 2, 1)

    arrived = onward(line)

    def part(blocks, state, last=False):
        return attend(use_warm, q, pos, blocks, state, last)

    held, state = [line], None
    half = nyh // 2
    for step in range(nz // 2 - 1):
        if step < nz // 2 - 2:
            coming = onward(arrived)
        else:
            coming = onward(lax.dynamic_slice_in_dim(arrived, (core * half).astype(jnp.uint32), half, axis=0))
        state = part([*held, arrived, handed(arrived)], state)
        arrived, state = lax.optimization_barrier((coming, state))
        held = []
    held = [arrived, handed(arrived)]
    slab_state = [pick(value, other_warm)[None] for value in state]
    slab = attend(jnp.ones(1, jnp.int32), q_other[None], pos, held, slab_state, True)
    slab, state = lax.optimization_barrier((slab, state))
    back = turn(slab[0], "yl", 2, 1)
    out = put(part(held, state, True), back, other_warm)
    out = lax.all_to_all(out, SECTION, 0, 0)
    return out.transpose(1, 0, 2).reshape(1, ROWS, H * HD)


def solution(mesh):
    sizes = {"x": 4, "yl": 2, "core": 2, "z": 8, "yh": 4}
    fine = Mesh(mesh.devices.reshape(tuple(sizes.values())), tuple(sizes))
    ctx = ("z", "yh")
    in_specs = (P(SECTION, ctx, None), P(SECTION, ctx, None, None), P(ctx), P())
    return jax.shard_map(
        functools.partial(per_device, sizes),
        mesh=fine,
        in_specs=in_specs,
        out_specs=P(SECTION, ctx, None),
        check_vma=False,
    )
```

```python
import functools

import jax
import jax.numpy as jnp
from jax import lax
from jax.experimental import pallas as pl
from jax.experimental.pallas import tpu as pltpu
from jax.sharding import Mesh, PartitionSpec as P

H = 32
KVH = 4
HD = 128
BLOCK = 64
WARM = 2
LAYERS = 16
ROWS = 128
HEADS = H // LAYERS
WIDE = HEADS * HD
SLABS = 8
POS_ROWS = 16
HALF_ROWS = 2 * ROWS + POS_ROWS
MASKED = -1e30
SCALE = 1.4426950408889634 / HD**0.5
SECTION = ("x", "yl", "core")


def attend_body(shards, first, last, *refs):
    it = iter(refs)
    warm_ref, q_ref, pos_ref = next(it), next(it), next(it)
    blocks = [next(it) for _ in shards]
    if not first:
        m_in, l_in, a_in = next(it), next(it), next(it)
    outs = [next(it)] if last else [next(it), next(it), next(it)]
    k, v, cap = it
    count = k.shape[1]
    row = lax.broadcasted_iota(jnp.int32, (BLOCK, ROWS), 0).astype(jnp.float32)
    at = 0
    for n, ref in zip(shards, blocks):
        for i in range(n):
            for source in range(2):
                base = source * ROWS
                k[source, at : at + ROWS, :] = ref[i, base : base + ROWS]
                v[source, :HD, at : at + ROWS] = ref[i, HALF_ROWS + base : HALF_ROWS + base + ROWS]
            ids = ref[i, 2 * ROWS : HALF_ROWS].astype(jnp.float32)
            for part in range(ROWS // BLOCK):
                key_pos = ids[0:1, part * BLOCK : part * BLOCK + 1] * BLOCK + row
                rows = slice(at + part * BLOCK, at + (part + 1) * BLOCK)
                cap[rows, :] = jnp.where(key_pos <= pos_ref[...], jnp.inf, MASKED)
            at += ROWS
    for source in range(2):
        v[source, HD:, :] = jnp.ones((POS_ROWS, count), jnp.bfloat16)

    def scores(j):
        q = jnp.concatenate([q_ref[j, :, h * HD : (h + 1) * HD] for h in range(HEADS)], axis=0)
        return lax.dot_general(
            k[warm_ref[j]], q, (((1,), (1,)), ((), ())), preferred_element_type=jnp.float32
        )

    def absorb(j, s):
        s = jnp.minimum(s, jnp.concatenate([cap[...]] * HEADS, axis=1))
        m = jnp.max(s, axis=0, keepdims=True)
        if not first:
            m_old = m_in[j, 0:1, :]
            m = jnp.maximum(m_old, m)
        w = jnp.exp2((s - m) * SCALE).astype(jnp.bfloat16)
        o = lax.dot_general(
            v[warm_ref[j]], w, (((1,), (0,)), ((), ())), preferred_element_type=jnp.float32
        )
        acc, den = o[:HD], o[HD : HD + 8]
        if not first:
            f = jnp.exp2((m_old - m) * SCALE)
            acc = acc + f * a_in[j]
            den = den + f * l_in[j]
        if last:
            done = acc / den[0:1]
            for h in range(HEADS):
                cols = slice(h * HD, (h + 1) * HD)
                outs[0][j, :, cols] = done[:, cols].T.astype(jnp.bfloat16)
        else:
            outs[0][j] = jnp.broadcast_to(m, den.shape)
            outs[1][j] = den
            outs[2][j] = acc

    slabs = min(SLABS, q_ref.shape[0])

    @pl.loop(0, q_ref.shape[0] // slabs)
    def _(step):
        base = step * slabs
        s = scores(base)
        for j in range(slabs):
            ahead = scores(base + j + 1) if j + 1 < slabs else None
            absorb(base + j, s)
            s = ahead


def attend(warm, q, pos, blocks, state, last):
    shards = tuple(b.shape[0] for b in blocks)
    count = sum(shards) * ROWS
    layers = q.shape[0]
    args = [warm, q, pos, *blocks]
    aliases = {}
    if state is not None:
        if not last:
            aliases = {len(args) + i: i for i in range(len(state))}
        args += list(state)
    whole = pl.BlockSpec(memory_space=pltpu.VMEM)
    one = jax.ShapeDtypeStruct((layers, 8, WIDE), jnp.float32)
    acc = jax.ShapeDtypeStruct((layers, HD, WIDE), jnp.float32)
    done = jax.ShapeDtypeStruct((layers, ROWS, WIDE), jnp.bfloat16)
    return pl.pallas_call(
        functools.partial(attend_body, shards, state is None, last),
        in_specs=[pl.BlockSpec(memory_space=pltpu.SMEM)] + [whole] * (len(args) - 1),
        out_specs=whole if last else [whole] * 3,
        out_shape=done if last else [one, one, acc],
        scratch_shapes=[
            pltpu.VMEM((2, count, HD), jnp.bfloat16),
            pltpu.VMEM((2, HD + POS_ROWS, count), jnp.bfloat16),
            pltpu.VMEM((count, ROWS), jnp.float32),
        ],
        input_output_aliases=aliases,
        compiler_params=pltpu.CompilerParams(vmem_limit_bytes=24 << 20),
        cost_estimate=pl.CostEstimate(
            flops=4 * ROWS * layers * HEADS * count * HD,
            bytes_accessed=8 << 20,
            transcendentals=ROWS * layers * HEADS * count,
        ),
        name="attend",
    )(*args)


def turn(value, axis, size, shift):
    return lax.ppermute(value, axis, [(i, (i + shift) % size) for i in range(size)])


def packed(kv):
    def body(kv_ref, out_ref):
        for h in range(KVH):
            k = kv_ref[:, 0, h * HD : (h + 1) * HD]
            v = kv_ref[:, 1, h * HD : (h + 1) * HD].T
            for yl in range(LAYERS // KVH // 2):
                out_ref[h * 4 + yl * 2] = k
                out_ref[h * 4 + yl * 2 + 1] = v

    return pl.pallas_call(
        body,
        in_specs=[pl.BlockSpec(memory_space=pltpu.VMEM)],
        out_specs=pl.BlockSpec(memory_space=pltpu.VMEM),
        out_shape=jax.ShapeDtypeStruct((LAYERS, ROWS, HD), jnp.bfloat16),
        name="pack",
    )(kv)


def pick(slabs, index):
    return lax.dynamic_index_in_dim(slabs, index.astype(jnp.uint32), 0, keepdims=False)


def put(slabs, slab, index):
    return lax.dynamic_update_index_in_dim(slabs, slab, index.astype(jnp.uint32), 0)


def per_device(sizes, queries, key_values, token_pos, layer_of_section):
    nz, nyh = sizes["z"], sizes["yh"]
    core, yl = lax.axis_index("core"), lax.axis_index("yl")
    ids = jnp.arange(LAYERS, dtype=jnp.int32)
    holder = jnp.sum(jnp.where(layer_of_section[None, :] == ids[:, None], ids[None, :], 0), axis=1)
    top_holder = holder[LAYERS - 1]
    warm, other_warm = jnp.where(yl == 0, holder[0], holder[1]), jnp.where(yl == 0, holder[1], holder[0])
    use_warm = ((ids == warm) | (ids == other_warm)).astype(jnp.int32)
    pos = token_pos.astype(jnp.float32)[None, :]
    block_ids = jnp.broadcast_to((token_pos // BLOCK).astype(jnp.bfloat16)[None, :], (POS_ROWS, ROWS))
    pieces = packed(key_values[0])
    pieces = lax.all_to_all(pieces, SECTION, 0, 0)
    q = queries[0].reshape(ROWS, LAYERS, WIDE).transpose(1, 0, 2)
    q, pieces, top_holder, warm, other_warm, use_warm, pos, block_ids = lax.optimization_barrier(
        (q, pieces, top_holder, warm, other_warm, use_warm, pos, block_ids)
    )
    shard = jnp.concatenate([pick(pieces, top_holder), pick(pieces, warm), block_ids], axis=0)
    mine = jnp.stack([shard] + [turn(shard, "yh", nyh, shift) for shift in range(1, nyh)])
    q, mine = lax.optimization_barrier((q, mine))
    q = lax.all_to_all(q, SECTION, 0, 0)
    q_other = turn(pick(q, other_warm), "yl", 2, 1)
    q = put(q, q_other, other_warm)
    theirs = turn(mine, "core", 2, 1)
    keys, values = jnp.where(core == 0, mine, theirs), jnp.where(core == 0, theirs, mine)
    line = jnp.concatenate([keys, values], axis=1)

    pairs = [(z, (z + 1) % nz) for z in range(nz)] + [(nz + z, nz + (z - 1) % nz) for z in range(nz)]

    def onward(value):
        return lax.ppermute(value, ("core", "z"), pairs)

    def handed(value):
        return turn(value, "core", 2, 1)

    arrived = onward(line)
    arrived, q, q_other = lax.optimization_barrier((arrived, q, q_other))

    def part(blocks, state, last=False):
        return attend(use_warm, q, pos, blocks, state, last)

    held, state = [line], None
    half = nyh // 2
    for step in range(nz // 2 - 1):
        if step < nz // 2 - 2:
            coming = onward(arrived)
        else:
            coming = onward(lax.dynamic_slice_in_dim(arrived, (core * half).astype(jnp.uint32), half, axis=0))
        state = part([*held, arrived, handed(arrived)], state)
        arrived, state = lax.optimization_barrier((coming, state))
        held = []
    held = [arrived, handed(arrived)]
    slab_state = [pick(value, other_warm)[None] for value in state]
    slab = attend(jnp.ones(1, jnp.int32), q_other[None], pos, held, slab_state, True)
    slab, state = lax.optimization_barrier((slab, state))
    back = turn(slab[0], "yl", 2, 1)
    out = put(part(held, state, True), back, other_warm)
    out = lax.all_to_all(out, SECTION, 0, 0)
    return out.transpose(1, 0, 2).reshape(1, ROWS, H * HD)


def solution(mesh):
    sizes = {"x": 4, "yl": 2, "core": 2, "z": 8, "yh": 4}
    fine = Mesh(mesh.devices.reshape(tuple(sizes.values())), tuple(sizes))
    ctx = ("z", "yh")
    in_specs = (P(SECTION, ctx, None), P(SECTION, ctx, None, None), P(ctx), P())
    return jax.shard_map(
        functools.partial(per_device, sizes),
        mesh=fine,
        in_specs=in_specs,
        out_specs=P(SECTION, ctx, None),
        check_vma=False,
    )
```

```python
import functools

import jax
import jax.numpy as jnp
from jax import lax
from jax.experimental import pallas as pl
from jax.experimental.pallas import tpu as pltpu
from jax.sharding import Mesh, PartitionSpec as P

H = 32
KVH = 4
HD = 128
BLOCK = 64
WARM = 2
LAYERS = 16
ROWS = 128
HEADS = H // LAYERS
WIDE = HEADS * HD
SLABS = 8
POS_ROWS = 16
HALF_ROWS = 2 * ROWS + POS_ROWS
MASKED = -1e30
SCALE = 1.4426950408889634 / HD**0.5
SECTION = ("x", "yl", "core")


def attend_body(shards, first, last, *refs):
    it = iter(refs)
    warm_ref, q_ref, pos_ref = next(it), next(it), next(it)
    blocks = [next(it) for _ in shards]
    if not first:
        m_in, l_in, a_in = next(it), next(it), next(it)
    outs = [next(it)] if last else [next(it), next(it), next(it)]
    k, v, cap = it
    count = k.shape[1]
    row = lax.broadcasted_iota(jnp.int32, (BLOCK, ROWS), 0).astype(jnp.float32)
    at = 0
    for n, ref in zip(shards, blocks):
        for i in range(n):
            for source in range(2):
                base = source * ROWS
                k[source, at : at + ROWS, :] = ref[i, base : base + ROWS]
                v[source, :HD, at : at + ROWS] = ref[i, HALF_ROWS + base : HALF_ROWS + base + ROWS]
            ids = ref[i, 2 * ROWS : HALF_ROWS].astype(jnp.float32)
            for part in range(ROWS // BLOCK):
                key_pos = ids[0:1, part * BLOCK : part * BLOCK + 1] * BLOCK + row
                rows = slice(at + part * BLOCK, at + (part + 1) * BLOCK)
                cap[rows, :] = jnp.where(key_pos <= pos_ref[...], jnp.inf, MASKED)
            at += ROWS
    for source in range(2):
        v[source, HD:, :] = jnp.ones((POS_ROWS, count), jnp.bfloat16)

    def scores(j):
        q = jnp.concatenate([q_ref[j, :, h * HD : (h + 1) * HD] for h in range(HEADS)], axis=0)
        return lax.dot_general(
            k[warm_ref[j]], q, (((1,), (1,)), ((), ())), preferred_element_type=jnp.float32
        )

    def absorb(j, s):
        s = jnp.minimum(s, jnp.concatenate([cap[...]] * HEADS, axis=1))
        m = jnp.max(s, axis=0, keepdims=True)
        if not first:
            m_old = m_in[j, 0:1, :]
            m = jnp.maximum(m_old, m)
        w = jnp.exp2((s - m) * SCALE).astype(jnp.bfloat16)
        o = lax.dot_general(
            v[warm_ref[j]], w, (((1,), (0,)), ((), ())), preferred_element_type=jnp.float32
        )
        acc, den = o[:HD], o[HD : HD + 8]
        if not first:
            f = jnp.exp2((m_old - m) * SCALE)
            acc = acc + f * a_in[j]
            den = den + f * l_in[j]
        if last:
            done = acc / den[0:1]
            for h in range(HEADS):
                cols = slice(h * HD, (h + 1) * HD)
                outs[0][j, :, cols] = done[:, cols].T.astype(jnp.bfloat16)
        else:
            outs[0][j] = jnp.broadcast_to(m, den.shape)
            outs[1][j] = den
            outs[2][j] = acc

    slabs = min(SLABS, q_ref.shape[0])

    @pl.loop(0, q_ref.shape[0] // slabs)
    def _(step):
        base = step * slabs
        s = scores(base)
        for j in range(slabs):
            ahead = scores(base + j + 1) if j + 1 < slabs else None
            absorb(base + j, s)
            s = ahead


def attend(warm, q, pos, blocks, state, last):
    shards = tuple(b.shape[0] for b in blocks)
    count = sum(shards) * ROWS
    layers = q.shape[0]
    args = [warm, q, pos, *blocks]
    aliases = {}
    if state is not None:
        if not last:
            aliases = {len(args) + i: i for i in range(len(state))}
        args += list(state)
    whole = pl.BlockSpec(memory_space=pltpu.VMEM)
    one = jax.ShapeDtypeStruct((layers, 8, WIDE), jnp.float32)
    acc = jax.ShapeDtypeStruct((layers, HD, WIDE), jnp.float32)
    done = jax.ShapeDtypeStruct((layers, ROWS, WIDE), jnp.bfloat16)
    return pl.pallas_call(
        functools.partial(attend_body, shards, state is None, last),
        in_specs=[pl.BlockSpec(memory_space=pltpu.SMEM)] + [whole] * (len(args) - 1),
        out_specs=whole if last else [whole] * 3,
        out_shape=done if last else [one, one, acc],
        scratch_shapes=[
            pltpu.VMEM((2, count, HD), jnp.bfloat16),
            pltpu.VMEM((2, HD + POS_ROWS, count), jnp.bfloat16),
            pltpu.VMEM((count, ROWS), jnp.float32),
        ],
        input_output_aliases=aliases,
        compiler_params=pltpu.CompilerParams(vmem_limit_bytes=24 << 20),
        cost_estimate=pl.CostEstimate(
            flops=4 * ROWS * layers * HEADS * count * HD,
            bytes_accessed=8 << 20,
            transcendentals=ROWS * layers * HEADS * count,
        ),
        name="attend",
    )(*args)


def turn(value, axis, size, shift):
    return lax.ppermute(value, axis, [(i, (i + shift) % size) for i in range(size)])


def packed(kv):
    def body(kv_ref, out_ref):
        for h in range(KVH):
            k = kv_ref[:, 0, h * HD : (h + 1) * HD]
            v = kv_ref[:, 1, h * HD : (h + 1) * HD].T
            for yl in range(LAYERS // KVH // 2):
                out_ref[h * 4 + yl * 2] = k
                out_ref[h * 4 + yl * 2 + 1] = v

    return pl.pallas_call(
        body,
        in_specs=[pl.BlockSpec(memory_space=pltpu.VMEM)],
        out_specs=pl.BlockSpec(memory_space=pltpu.VMEM),
        out_shape=jax.ShapeDtypeStruct((LAYERS, ROWS, HD), jnp.bfloat16),
        name="pack",
    )(kv)


def pick(slabs, index):
    return lax.dynamic_index_in_dim(slabs, index.astype(jnp.uint32), 0, keepdims=False)


def put(slabs, slab, index):
    return lax.dynamic_update_index_in_dim(slabs, slab, index.astype(jnp.uint32), 0)


def per_device(sizes, queries, key_values, token_pos, layer_of_section):
    nz, nyh = sizes["z"], sizes["yh"]
    core, yl = lax.axis_index("core"), lax.axis_index("yl")
    ids = jnp.arange(LAYERS, dtype=jnp.int32)
    holder = jnp.sum(jnp.where(layer_of_section[None, :] == ids[:, None], ids[None, :], 0), axis=1)
    top_holder = holder[LAYERS - 1]
    warm, other_warm = jnp.where(yl == 0, holder[0], holder[1]), jnp.where(yl == 0, holder[1], holder[0])
    use_warm = ((ids == warm) | (ids == other_warm)).astype(jnp.int32)
    pos = token_pos.astype(jnp.float32)[None, :]
    block_ids = jnp.broadcast_to((token_pos // BLOCK).astype(jnp.bfloat16)[None, :], (POS_ROWS, ROWS))
    pieces = packed(key_values[0])
    pieces = lax.all_to_all(pieces, SECTION, 0, 0)
    q = queries[0].reshape(ROWS, LAYERS, WIDE).transpose(1, 0, 2)
    q, pieces, top_holder, warm, other_warm, use_warm, pos, block_ids = lax.optimization_barrier(
        (q, pieces, top_holder, warm, other_warm, use_warm, pos, block_ids)
    )
    shard = jnp.concatenate([pick(pieces, top_holder), pick(pieces, warm), block_ids], axis=0)
    others = [turn(shard, "yh", nyh, shift) for shift in range(1, nyh)]
    q, others[0] = lax.optimization_barrier((q, others[0]))
    mine = jnp.stack([shard, *others])
    q = lax.all_to_all(q, SECTION, 0, 0)
    q_other = turn(pick(q, other_warm), "yl", 2, 1)
    q = put(q, q_other, other_warm)
    theirs = turn(mine, "core", 2, 1)
    keys, values = jnp.where(core == 0, mine, theirs), jnp.where(core == 0, theirs, mine)
    line = jnp.concatenate([keys, values], axis=1)

    pairs = [(z, (z + 1) % nz) for z in range(nz)] + [(nz + z, nz + (z - 1) % nz) for z in range(nz)]

    def onward(value):
        return lax.ppermute(value, ("core", "z"), pairs)

    def handed(value):
        return turn(value, "core", 2, 1)

    arrived = onward(line)
    arrived, q, q_other = lax.optimization_barrier((arrived, q, q_other))

    def part(blocks, state, last=False):
        return attend(use_warm, q, pos, blocks, state, last)

    held, state = [line], None
    half = nyh // 2
    for step in range(nz // 2 - 1):
        if step < nz // 2 - 2:
            coming = onward(arrived)
        else:
            coming = onward(lax.dynamic_slice_in_dim(arrived, (core * half).astype(jnp.uint32), half, axis=0))
        state = part([*held, arrived, handed(arrived)], state)
        arrived, state = lax.optimization_barrier((coming, state))
        held = []
    held = [arrived, handed(arrived)]
    slab_state = [pick(value, other_warm)[None] for value in state]
    slab = attend(jnp.ones(1, jnp.int32), q_other[None], pos, held, slab_state, True)
    slab, state = lax.optimization_barrier((slab, state))
    back = turn(slab[0], "yl", 2, 1)
    out = put(part(held, state, True), back, other_warm)
    out = lax.all_to_all(out, SECTION, 0, 0)
    return out.transpose(1, 0, 2).reshape(1, ROWS, H * HD)


def solution(mesh):
    sizes = {"x": 4, "yl": 2, "core": 2, "z": 8, "yh": 4}
    fine = Mesh(mesh.devices.reshape(tuple(sizes.values())), tuple(sizes))
    ctx = ("z", "yh")
    in_specs = (P(SECTION, ctx, None), P(SECTION, ctx, None, None), P(ctx), P())
    return jax.shard_map(
        functools.partial(per_device, sizes),
        mesh=fine,
        in_specs=in_specs,
        out_specs=P(SECTION, ctx, None),
        check_vma=False,
    )
```
